256 devices in a mesh: depth: 8 (over z), row: 4 (over y), col: 8 (over x, core).
Axes of the slice: x: 4, y: 4, z: 8, core: 2. Of those that a mesh axis runs over, the one named last changes fastest.
Arguments:
- density: bfloat16 [64, 512, 2048], P('depth', 'row', 'col'), may hold values from 0.0046691895 to 0.09375
- emission: bfloat16 [3, 64, 512, 2048], P(None, 'depth', 'row', 'col'), may hold values from 0.19921875 to 5
- offsets: int32 [3, 2, 8, 4, 16], P(None, None, 'depth', 'row', 'col'), may hold values from -8 to 8
- view_order: int32 [3, 4], P(None, 'row'), may hold values from 0 to 1
Outputs:
- image: float32 [3, 4, 64, 8, 2048], P(None, None, 'row', 'depth', 'col')
The draws below stay inside these ranges and needn't reach their ends.
Inputs may be any that keep to these rules, and one draw needn't show every extreme that they name: `offsets`: displacement in cells of each brick's footprint from its home position in each view. `view_order`: 1 reverses the rays' direction along depth in that view and band of brick rows.
All inputs are finite; a program needn't handle non-finite values.
Results may differ from the reference program's by a relative error of at most 0.00052.
Values sent between devices are 32-bit elements; how exact they have to be, the bound alone decides.
A program may use at most 128 MiB of HBM per device.

```python
import math
import jax
import jax.numpy as jnp
from jax import lax

BL = 128
MARGIN = 16
JIT = 8
BZ = 8
VIEWS = 3
TILE = 160
SLABS = 8
BROWS = 4
BCOLS = 16
ZCELLS = 64
YCELLS = 512
XCELLS = 2048


def place_ends(values, key, least, high):
    shape = values.shape
    spot = [jax.random.randint(jax.random.fold_in(key, axis), (), 0, shape[axis]) for axis in range(len(shape))]
    values = values.at[tuple(spot)].set(least)
    longest = shape.index(max(shape))
    spot[longest] = (spot[longest] + 1) % shape[longest]
    return values.at[tuple(spot)].set(high)


def block_scale(stream_key, shape, shards, smallest, largest):
    gain = 1.0
    for axis_at, parts in shards:
        heights = jax.random.uniform(jax.random.fold_in(jax.random.fold_in(stream_key, 6), axis_at), (parts,), jnp.float32, smallest / len(shards), largest / len(shards))
        gain = gain * jnp.repeat(jnp.exp(heights), shape[axis_at] // parts).reshape((-1,) + (1,) * (len(shape) - 1 - axis_at))
    return gain


def setup_inputs(seed: int = 0) -> dict:
    splits = jax.random.split(jax.random.key(seed), 5)
    return {
        "density": jnp.clip(jnp.exp(math.log(0.09375) - 2.9996462 * jax.random.uniform(splits[0], (ZCELLS, YCELLS, XCELLS), jnp.float32) ** block_scale(splits[0], (ZCELLS, YCELLS, XCELLS), ((0, 8), (1, 4), (2, 8)), -0.2, 0.2)), 0.0046691895, 0.09375).astype(jnp.bfloat16),
        "emission": jnp.clip(jnp.exp(math.log(5.0) - 3.2227897 * jax.random.uniform(splits[1], (3, ZCELLS, YCELLS, XCELLS), jnp.float32) ** block_scale(splits[1], (3, ZCELLS, YCELLS, XCELLS), ((1, 8), (2, 4), (3, 8)), -0.2, 0.2)), 0.19921875, 5.0).astype(jnp.bfloat16),
        "offsets": place_ends(jax.random.randint(splits[2], (VIEWS, 2, SLABS, BROWS, BCOLS), 0 - JIT, JIT + 1), jax.random.fold_in(splits[2], 1), 0 - JIT, JIT).astype(jnp.int32),
        "view_order": place_ends(jax.random.randint(splits[3], (VIEWS, BROWS), 0, 2), jax.random.fold_in(splits[3], 1), 0, 1).astype(jnp.int32),
    }


SHEAR_ROWS = (0.75, -0.5, 0.25)
SHEAR_COLS = (-0.25, 0.625, -0.875)


def bilinear(shear_rate, slices, length, margin):
    tile_width = length + 2 * margin
    slice_pos = jnp.arange(slices, dtype=jnp.float32)
    slice_shift = shear_rate * (margin - 2) * (2.0 * slice_pos - (slices - 1)) / slices
    target = jnp.arange(tile_width, dtype=jnp.float32)
    source = jnp.arange(length, dtype=jnp.float32)
    distance = target[None, :, None] - margin - slice_shift[:, None, None] - source[None, None, :]
    return jnp.maximum(0.0, 1.0 - jnp.abs(distance)).astype(jnp.bfloat16)


def integrate(footprint, backward):
    extinction = footprint[0]
    running = jnp.cumsum(extinction, axis=-3)
    total_depth = jnp.sum(extinction, axis=-3)
    prefix_depth = jnp.where(backward, total_depth[..., None, :, :] - running, running - extinction)
    weight = (1.0 - jnp.exp(-extinction)) * jnp.exp(-prefix_depth)
    colors = jnp.sum(footprint[1:] * weight, axis=-3)
    return jnp.concatenate([colors, total_depth[None]], 0)


def pad_along(source_array, lead_count, trail_count, axis_pos):
    widths = [(0, 0)] * source_array.ndim
    widths[axis_pos] = (lead_count, trail_count)
    return jnp.pad(source_array, widths)


def wrap_fold(canvas, rim_width, cell_count, axis_pos):
    interior = lax.slice_in_dim(canvas, rim_width, rim_width + cell_count, axis=axis_pos)
    head_rim = lax.slice_in_dim(canvas, 0, rim_width, axis=axis_pos)
    tail_rim = lax.slice_in_dim(canvas, rim_width + cell_count, cell_count + 2 * rim_width, axis=axis_pos)
    return interior + pad_along(head_rim, cell_count - rim_width, 0, axis_pos) + pad_along(tail_rim, 0, cell_count - rim_width, axis_pos)


def composite(slab_images, backward):
    depth_parts = slab_images[:, 3]
    running = jnp.cumsum(depth_parts, axis=0)
    depth_sum = running[-1]
    prefix_depth = jnp.where(backward, depth_sum[None] - running, running - depth_parts)
    colors = jnp.sum(slab_images[:, :3] * jnp.exp(-prefix_depth)[:, None], axis=0)
    return jnp.concatenate([colors, jnp.exp(-depth_sum)[None]], 0)


def reference(density, emission, offsets, view_order):
    fields = jnp.concatenate([density[None], emission], 0)
    rim_width = MARGIN + JIT
    per_view = []
    for view_index in range(VIEWS):
        row_weights = bilinear(SHEAR_ROWS[view_index], BZ, BL, MARGIN).astype(jnp.float32)
        col_weights = bilinear(SHEAR_COLS[view_index], BZ, BL, MARGIN).astype(jnp.float32)
        band_orders = view_order[view_index]

        def deposit(canvas, brick_flat):
            slab_index = brick_flat // (BROWS * BCOLS)
            remainder = brick_flat % (BROWS * BCOLS)
            brick_row = remainder // BCOLS
            brick_col = remainder % BCOLS
            brick_cells = lax.dynamic_slice(
                fields,
                (jnp.int32(0), (slab_index * BZ).astype(jnp.int32), (brick_row * BL).astype(jnp.int32), (brick_col * BL).astype(jnp.int32)),
                (4, BZ, BL, BL))
            resampled = jnp.einsum("fzyx,zux->fzyu", brick_cells.astype(jnp.float32), col_weights).astype(jnp.bfloat16)
            footprint = jnp.einsum("zty,fzyu->fztu", row_weights, resampled.astype(jnp.float32))
            shaded = integrate(footprint, band_orders[brick_row] == 1)
            top_row = (brick_row * BL + offsets[view_index, 0, slab_index, brick_row, brick_col] + JIT).astype(jnp.int32)
            left_col = (brick_col * BL + offsets[view_index, 1, slab_index, brick_row, brick_col] + JIT).astype(jnp.int32)
            corner = (slab_index.astype(jnp.int32), jnp.int32(0), top_row, left_col)
            current = lax.dynamic_slice(canvas, corner, (1, 4, TILE, TILE))
            return lax.dynamic_update_slice(canvas, current + shaded[None], corner), None

        canvas = jnp.zeros((SLABS, 4, YCELLS + 2 * rim_width, XCELLS + 2 * rim_width), jnp.float32)
        canvas, unused = lax.scan(deposit, canvas, jnp.arange(SLABS * BROWS * BCOLS, dtype=jnp.int32))
        slab_images = wrap_fold(wrap_fold(canvas, rim_width, YCELLS, 2), rim_width, XCELLS, 3)
        row_backward = (jnp.repeat(band_orders, BL) == 1)[:, None]
        per_view.append(composite(slab_images, row_backward))
    image_all = jnp.stack(per_view)
    return image_all.reshape(VIEWS, 4, YCELLS // SLABS, SLABS, XCELLS)
```

```python
import functools

import jax
import jax.numpy as jnp
from jax import lax
from jax.experimental import pallas as pl
from jax.experimental.pallas import tpu as pltpu
from jax.sharding import PartitionSpec as P

MESH = pl.DeviceIdType.MESH
VIEWS = 3
MARGIN = 16
JIT = 8
SLICES = 8
LEN = 128
SHEAR_ROWS = (0.75, -0.5, 0.25)
SHEAR_COLS = (-0.25, 0.625, -0.875)
RIMS = tuple(
    -(-int(abs(a) * (MARGIN - 2) * (SLICES - 1) / SLICES + 1 + JIT) // 8) * 8 for a in SHEAR_ROWS
)
RIM = max(RIMS)
TALL = LEN + 2 * RIM
SLOT = 32

ROW_UP, ROW_DOWN, COL_LEFT, COL_RIGHT, UP_LEFT, UP_RIGHT, DOWN_LEFT, DOWN_RIGHT = range(8)


def shift_of(rate, z):
    return rate * (MARGIN - 2) / SLICES * (2.0 * z - (SLICES - 1))


def tent(distance):
    return jnp.maximum(0.0, 1.0 - jnp.abs(distance)).astype(jnp.bfloat16)


def kernel(
    sections, bands, stripes,
    density, emission, offsets, orders, out,
    foot, image, left, right,
    from_row, from_col, from_corner, sent, got_0, got_1, got_2,
    send_rim, recv_rim, send_depth, recv_depth,
):
    got = (got_0, got_1, got_2)
    me = lax.axis_index("depth")
    band = lax.axis_index("row")
    stripe = lax.axis_index("col")

    def place(drow, dcol):
        return {
            "row": lax.rem(band + drow + bands, bands),
            "col": lax.rem(stripe + dcol + stripes, stripes),
        }

    around = {
        ROW_UP: place(-1, 0), ROW_DOWN: place(1, 0), COL_LEFT: place(0, -1), COL_RIGHT: place(0, 1),
        UP_LEFT: place(-1, -1), UP_RIGHT: place(-1, 1), DOWN_LEFT: place(1, -1), DOWN_RIGHT: place(1, 1),
    }
    barrier = pltpu.get_barrier_semaphore()
    for device in around.values():
        pl.semaphore_signal(barrier, inc=1, device_id=device, device_id_type=MESH)
    for hop in range(1, sections):
        pl.semaphore_signal(
            barrier, inc=1, device_id={"depth": lax.rem(me + hop, sections)}, device_id_type=MESH
        )

    lane = lax.broadcasted_iota(jnp.int32, (LEN, 2 * LEN), 1)
    cell = lax.broadcasted_iota(jnp.int32, (LEN, 2 * LEN), 0)
    tail = lane - LEN
    nowhere = -4096
    column = (
        jnp.where(lane < LEN, lane, jnp.where(tail < SLOT, tail + LEN,
                  jnp.where(tail < 2 * SLOT, tail - 2 * SLOT, nowhere))),
        jnp.where(lane < LEN, lane, jnp.where(tail < 2 * SLOT, nowhere,
                  jnp.where(tail < 3 * SLOT, tail + LEN - 2 * SLOT, tail - LEN))),
    )
    col_base = [(c - cell).astype(jnp.float32) for c in column]
    tile_lane = lax.broadcasted_iota(jnp.int32, (8, LEN), 1)

    def resample(view):
        rim = RIMS[view]
        tall = LEN + 2 * rim
        row_base = (
            lax.broadcasted_iota(jnp.int32, (tall, LEN), 0) - rim
            - lax.broadcasted_iota(jnp.int32, (tall, LEN), 1)
        ).astype(jnp.float32)

        def slice_body(z, carry):
            zf = z.astype(jnp.float32)
            tails, row_weights = [], []
            for b in range(2):
                oy = offsets[view * 4 + b].astype(jnp.float32)
                ox = offsets[view * 4 + 2 + b].astype(jnp.float32)
                cols = slice(b * LEN, (b + 1) * LEN)
                cells = jnp.concatenate(
                    [density[z, :, cols]] + [emission[c, z, :, cols] for c in range(3)], 0
                )
                col_weights = tent(col_base[b] - (ox + shift_of(SHEAR_COLS[view], zf)))
                lines = jnp.dot(
                    cells, col_weights, preferred_element_type=jnp.float32
                ).astype(jnp.bfloat16)
                rw = tent(row_base - (oy + shift_of(SHEAR_ROWS[view], zf)))
                own = jnp.concatenate([lines[f * LEN:(f + 1) * LEN, :LEN] for f in range(4)], 1)
                tails.append(
                    jnp.concatenate([lines[f * LEN:(f + 1) * LEN, LEN:] for f in range(4)], 1)
                )
                row_weights.append(rw)
                prints = jnp.dot(rw, own, preferred_element_type=jnp.float32)
                for f in range(4):
                    foot[b, z, f, 0:tall, :] = prints[:, f * LEN:(f + 1) * LEN]
            prints = jnp.dot(
                jnp.concatenate(row_weights, 1), jnp.concatenate(tails, 0),
                preferred_element_type=jnp.float32,
            )
            for f in range(4):
                foot[2, z, f, 0:tall, :] = prints[:, f * LEN:(f + 1) * LEN]
            return carry

        lax.fori_loop(0, SLICES, slice_body, 0)

    def shade(view):
        rim = RIMS[view]
        tall = LEN + 2 * rim
        backward = orders[view]
        steps = [z + backward * (SLICES - 1 - 2 * z) for z in range(SLICES)]

        def integrate(region, rows):
            through = jnp.ones((8, LEN), jnp.float32)
            depth = jnp.zeros((8, LEN), jnp.float32)
            colors = [jnp.zeros((8, LEN), jnp.float32) for _ in range(3)]
            for z in steps:
                e = foot[region, z, 0, rows, :]
                after = through * jnp.exp(-e)
                weight = through - after
                through = after
                depth += e
                for c in range(3):
                    colors[c] += foot[region, z, 1 + c, rows, :] * weight
            return colors + [depth]

        def row_body(i, carry):
            rows = pl.ds(pl.multiple_of(i * 8, 8), 8)
            rims = integrate(2, rows)
            lefts = jnp.zeros((8, LEN), jnp.float32)
            rights = jnp.zeros((8, LEN), jnp.float32)
            for c in range(4):
                mine = jnp.where((tile_lane >= SLOT) & (tile_lane < 2 * SLOT), rims[c], 0.0)
                lefts += pltpu.roll(mine, (SLOT * c - SLOT) % LEN, 1)
                mine = jnp.where((tile_lane >= 2 * SLOT) & (tile_lane < 3 * SLOT), rims[c], 0.0)
                rights += pltpu.roll(mine, (SLOT * c - 2 * SLOT) % LEN, 1)
            left[view, rows, :] = lefts
            right[view, rows, :] = rights
            first = integrate(0, rows)
            for c in range(4):
                image[view, 0, c, rows, :] = first[c] + jnp.where(tile_lane >= 3 * SLOT, rims[c], 0.0)
            second = integrate(1, rows)
            for c in range(4):
                image[view, 1, c, rows, :] = second[c] + jnp.where(tile_lane < SLOT, rims[c], 0.0)
            return carry

        lax.fori_loop(0, tall // 8, row_body, 0)

    def rim_copies(view):
        rim = RIMS[view]
        top, mid, low = pl.ds(0, rim), pl.ds(rim, LEN), pl.ds(rim + LEN, rim)
        near = pl.ds(0, rim)
        moves = {
            ROW_UP: (image.at[view, :, :, top, :], from_row.at[view, 0, :, :, near, :]),
            ROW_DOWN: (image.at[view, :, :, low, :], from_row.at[view, 1, :, :, near, :]),
            COL_LEFT: (left.at[view, mid, :], from_col.at[view, 0]),
            COL_RIGHT: (right.at[view, mid, :], from_col.at[view, 1]),
            UP_LEFT: (left.at[view, top, :], from_corner.at[view, 0, near, :]),
            UP_RIGHT: (right.at[view, top, :], from_corner.at[view, 1, near, :]),
            DOWN_LEFT: (left.at[view, low, :], from_corner.at[view, 2, near, :]),
            DOWN_RIGHT: (right.at[view, low, :], from_corner.at[view, 3, near, :]),
        }
        return [
            pltpu.make_async_remote_copy(
                src_ref=src, dst_ref=dst,
                send_sem=send_rim.at[view, way], recv_sem=recv_rim.at[view, way],
                device_id=around[way], device_id_type=MESH,
            )
            for way, (src, dst) in moves.items()
        ]

    def fold(view):
        rim = RIMS[view]
        tiles = LEN // 8
        for i in range(tiles):
            rows = slice(rim + i * 8, rim + i * 8 + 8)
            here = slice(i * 8, i * 8 + 8)
            from_right = from_col[view, 0, here, :]
            from_left = from_col[view, 1, here, :]
            above = i * 8 < rim
            below = i * 8 >= LEN - rim
            if above:
                from_right += from_corner[view, 2, here, :]
                from_left += from_corner[view, 3, here, :]
            if below:
                lows = slice(i * 8 - (LEN - rim), i * 8 - (LEN - rim) + 8)
                from_right += from_corner[view, 0, lows, :]
                from_left += from_corner[view, 1, lows, :]
            for c in range(4):
                own = [image[view, b, c, rows, :] for b in range(2)]
                own[0] += jnp.where(
                    tile_lane < SLOT, pltpu.roll(from_left, (-SLOT * c) % LEN, 1), 0.0
                )
                own[1] += jnp.where(
                    tile_lane >= LEN - SLOT,
                    pltpu.roll(from_right, (LEN - SLOT - SLOT * c) % LEN, 1), 0.0,
                )
                for b in range(2):
                    if above:
                        own[b] += from_row[view, 1, b, c, here, :]
                    if below:
                        own[b] += from_row[view, 0, b, c, lows, :]
                    image[view, b, c, rows, :] = own[b]
        for k in range(sections):
            for c in range(4):
                for b in range(2):
                    sent[view, k, b, c] = image[
                        view, b, c, pl.ds(rim + k, LEN // sections, stride=sections), :
                    ]

    def depth_copies(view):
        copies = []
        for hop in range(1, sections):
            other = lax.rem(me + hop, sections)
            copies.append(
                pltpu.make_async_remote_copy(
                    src_ref=sent.at[view, other], dst_ref=got[view].at[hop],
                    send_sem=send_depth.at[view, hop], recv_sem=recv_depth.at[view, hop],
                    device_id={"depth": other}, device_id_type=MESH,
                )
            )
        return copies

    def composite(view):
        got[view][0] = sent[view, me]
        backward = orders[view]
        rows = LEN // sections
        for b in range(2):
            cols = slice(b * LEN, (b + 1) * LEN)
            through = jnp.ones((rows, LEN), jnp.float32)
            colors = [jnp.zeros((rows, LEN), jnp.float32) for _ in range(3)]
            for step in range(sections):
                slab = step + backward * (sections - 1 - 2 * step)
                slot = lax.rem(me - slab + sections, sections)
                for c in range(3):
                    colors[c] += got[view][slot, b, c] * through
                through = through * jnp.exp(-got[view][slot, b, 3])
            for c in range(3):
                out[view, c, :, cols] = colors[c]
            out[view, 3, :, cols] = through

    rim_sends, depth_sends = [], []
    for view in range(VIEWS):
        resample(view)
        shade(view)
        if view == 0:
            pl.semaphore_wait(barrier, 8 + sections - 1)
        rim_sends.append(rim_copies(view))
        for copy in rim_sends[view]:
            copy.start()
        if view > 0:
            for copy in rim_sends[view - 1]:
                copy.wait()
            fold(view - 1)
            depth_sends.append(depth_copies(view - 1))
            for copy in depth_sends[view - 1]:
                copy.start()
    for copy in rim_sends[VIEWS - 1]:
        copy.wait()
    fold(VIEWS - 1)
    depth_sends.append(depth_copies(VIEWS - 1))
    for copy in depth_sends[VIEWS - 1]:
        copy.start()
    for view in range(VIEWS):
        for copy in depth_sends[view]:
            copy.wait()
        composite(view)


def local(density, emission, offsets, view_order, sections, bands, stripes):
    rows, columns = LEN // sections, 2 * LEN
    vmem, smem = pl.BlockSpec(memory_space=pltpu.VMEM), pl.BlockSpec(memory_space=pltpu.SMEM)
    image = pl.pallas_call(
        functools.partial(kernel, sections, bands, stripes),
        out_shape=jax.ShapeDtypeStruct((VIEWS, 4, rows, columns), jnp.float32),
        in_specs=[vmem, vmem, smem, smem],
        out_specs=vmem,
        scratch_shapes=[
            pltpu.VMEM((3, SLICES, 4, TALL, LEN), jnp.float32),
            pltpu.VMEM((VIEWS, 2, 4, TALL, LEN), jnp.float32),
            pltpu.VMEM((VIEWS, TALL, LEN), jnp.float32),
            pltpu.VMEM((VIEWS, TALL, LEN), jnp.float32),
            pltpu.VMEM((VIEWS, 2, 2, 4, RIM, LEN), jnp.float32),
            pltpu.VMEM((VIEWS, 2, LEN, LEN), jnp.float32),
            pltpu.VMEM((VIEWS, 4, RIM, LEN), jnp.float32),
            pltpu.VMEM((VIEWS, sections, 2, 4, rows, LEN), jnp.float32),
            pltpu.VMEM((sections, 2, 4, rows, LEN), jnp.float32),
            pltpu.VMEM((sections, 2, 4, rows, LEN), jnp.float32),
            pltpu.VMEM((sections, 2, 4, rows, LEN), jnp.float32),
            pltpu.SemaphoreType.DMA((VIEWS, 8)),
            pltpu.SemaphoreType.DMA((VIEWS, 8)),
            pltpu.SemaphoreType.DMA((VIEWS, sections)),
            pltpu.SemaphoreType.DMA((VIEWS, sections)),
        ],
        compiler_params=pltpu.CompilerParams(
            collective_id=0, has_side_effects=True, vmem_limit_bytes=48 * 1024 * 1024
        ),
    )(density, emission, offsets.reshape(-1), view_order.reshape(-1))
    return image.reshape(VIEWS, 4, rows, 1, columns)


def solution(mesh):
    return jax.shard_map(
        functools.partial(
            local, sections=mesh.shape["depth"], bands=mesh.shape["row"], stripes=mesh.shape["col"]
        ),
        mesh=mesh,
        in_specs=(
            P("depth", "row", "col"),
            P(None, "depth", "row", "col"),
            P(None, None, "depth", "row", "col"),
            P(None, "row"),
        ),
        out_specs=P(None, None, "row", "depth", "col"),
        check_vma=False,
    )
```

```python
import functools

import jax
import jax.numpy as jnp
from jax import lax
from jax.experimental import pallas as pl
from jax.experimental.pallas import tpu as pltpu
from jax.sharding import PartitionSpec as P

MESH = pl.DeviceIdType.MESH
VIEWS = 3
MARGIN = 16
JIT = 8
SLICES = 8
LEN = 128
SHEAR_ROWS = (0.75, -0.5, 0.25)
SHEAR_COLS = (-0.25, 0.625, -0.875)
RIMS = tuple(
    -(-int(abs(a) * (MARGIN - 2) * (SLICES - 1) / SLICES + 1 + JIT) // 8) * 8 for a in SHEAR_ROWS
)
RIM = max(RIMS)
TALL = LEN + 2 * RIM
SLOT = 32

ROW_UP, ROW_DOWN, COL_LEFT, COL_RIGHT, UP_LEFT, UP_RIGHT, DOWN_LEFT, DOWN_RIGHT = range(8)


def shift_of(rate, z):
    return rate * (MARGIN - 2) / SLICES * (2.0 * z - (SLICES - 1))


def tent(distance):
    return jnp.maximum(0.0, 1.0 - jnp.abs(distance)).astype(jnp.bfloat16)


def kernel(
    sections, bands, stripes,
    density_hbm, emission_hbm, offsets, orders, out,
    density, emission, foot, image, left, right,
    from_row, from_col, from_corner, sent, raw, got_0, got_1, got_2,
    load_sem, send_rim, recv_rim, send_near, recv_near, send_far, recv_far,
):
    loads = (
        pltpu.make_async_copy(density_hbm, density, load_sem.at[0]),
        pltpu.make_async_copy(emission_hbm, emission, load_sem.at[1]),
    )
    for load in loads:
        load.start()
    got = (got_0, got_1, got_2)
    me = lax.axis_index("depth")
    odd = lax.rem(me, 2)
    sign = 1 - 2 * odd
    partner = me + sign
    band = lax.axis_index("row")
    stripe = lax.axis_index("col")

    def place(drow, dcol):
        return {
            "row": lax.rem(band + drow + bands, bands),
            "col": lax.rem(stripe + dcol + stripes, stripes),
        }

    around = {
        ROW_UP: place(-1, 0), ROW_DOWN: place(1, 0), COL_LEFT: place(0, -1), COL_RIGHT: place(0, 1),
        UP_LEFT: place(-1, -1), UP_RIGHT: place(-1, 1), DOWN_LEFT: place(1, -1), DOWN_RIGHT: place(1, 1),
    }
    barrier = pltpu.get_barrier_semaphore()
    for device in around.values():
        pl.semaphore_signal(barrier, inc=1, device_id=device, device_id_type=MESH)
    for hop in range(1, sections):
        pl.semaphore_signal(
            barrier, inc=1, device_id={"depth": lax.rem(me + hop, sections)}, device_id_type=MESH
        )

    lane = lax.broadcasted_iota(jnp.int32, (LEN, 2 * LEN), 1)
    cell = lax.broadcasted_iota(jnp.int32, (LEN, 2 * LEN), 0)
    tail = lane - LEN
    nowhere = -4096
    column = (
        jnp.where(lane < LEN, lane, jnp.where(tail < SLOT, tail + LEN,
                  jnp.where(tail < 2 * SLOT, tail - 2 * SLOT, nowhere))),
        jnp.where(lane < LEN, lane, jnp.where(tail < 2 * SLOT, nowhere,
                  jnp.where(tail < 3 * SLOT, tail + LEN - 2 * SLOT, tail - LEN))),
    )
    col_base = [(c - cell).astype(jnp.float32) for c in column]
    tile_lane = lax.broadcasted_iota(jnp.int32, (8, LEN), 1)

    def resample(view):
        rim = RIMS[view]
        tall = LEN + 2 * rim
        row_base = (
            lax.broadcasted_iota(jnp.int32, (tall, LEN), 0) - rim
            - lax.broadcasted_iota(jnp.int32, (tall, LEN), 1)
        ).astype(jnp.float32)

        def slice_body(z, carry):
            zf = z.astype(jnp.float32)
            tails, row_weights = [], []
            for b in range(2):
                oy = offsets[view, 0, 0, 0, b].astype(jnp.float32)
                ox = offsets[view, 1, 0, 0, b].astype(jnp.float32)
                cols = slice(b * LEN, (b + 1) * LEN)
                cells = jnp.concatenate(
                    [density[z, :, cols]] + [emission[c, z, :, cols] for c in range(3)], 0
                )
                col_weights = tent(col_base[b] - (ox + shift_of(SHEAR_COLS[view], zf)))
                lines = jnp.dot(
                    cells, col_weights, preferred_element_type=jnp.float32
                ).astype(jnp.bfloat16)
                rw = tent(row_base - (oy + shift_of(SHEAR_ROWS[view], zf)))
                own = jnp.concatenate([lines[f * LEN:(f + 1) * LEN, :LEN] for f in range(4)], 1)
                tails.append(
                    jnp.concatenate([lines[f * LEN:(f + 1) * LEN, LEN:] for f in range(4)], 1)
                )
                row_weights.append(rw)
                prints = jnp.dot(rw, own, preferred_element_type=jnp.float32)
                for f in range(4):
                    foot[b, z, f, 0:tall, :] = prints[:, f * LEN:(f + 1) * LEN]
            prints = jnp.dot(
                jnp.concatenate(row_weights, 1), jnp.concatenate(tails, 0),
                preferred_element_type=jnp.float32,
            )
            for f in range(4):
                foot[2, z, f, 0:tall, :] = prints[:, f * LEN:(f + 1) * LEN]
            return carry

        lax.fori_loop(0, SLICES, slice_body, 0, unroll=4)

    def shade(view):
        rim = RIMS[view]
        tall = LEN + 2 * rim
        backward = orders[view, 0]
        steps = [z + backward * (SLICES - 1 - 2 * z) for z in range(SLICES)]

        def integrate(region, rows):
            through = jnp.ones((8, LEN), jnp.float32)
            depth = jnp.zeros((8, LEN), jnp.float32)
            colors = [jnp.zeros((8, LEN), jnp.float32) for _ in range(3)]
            for z in steps:
                e = foot[region, z, 0, rows, :]
                after = through * jnp.exp(-e)
                weight = through - after
                through = after
                depth += e
                for c in range(3):
                    colors[c] += foot[region, z, 1 + c, rows, :] * weight
            return colors + [depth]

        def row_body(i, carry):
            rows = pl.ds(pl.multiple_of(i * 8, 8), 8)
            rims = integrate(2, rows)
            lefts = jnp.zeros((8, LEN), jnp.float32)
            rights = jnp.zeros((8, LEN), jnp.float32)
            for c in range(4):
                mine = jnp.where((tile_lane >= SLOT) & (tile_lane < 2 * SLOT), rims[c], 0.0)
                lefts += pltpu.roll(mine, (SLOT * c - SLOT) % LEN, 1)
                mine = jnp.where((tile_lane >= 2 * SLOT) & (tile_lane < 3 * SLOT), rims[c], 0.0)
                rights += pltpu.roll(mine, (SLOT * c - 2 * SLOT) % LEN, 1)
            left[view, rows, :] = lefts
            right[view, rows, :] = rights
            first = integrate(0, rows)
            for c in range(4):
                image[view, 0, c, rows, :] = first[c] + jnp.where(tile_lane >= 3 * SLOT, rims[c], 0.0)
            second = integrate(1, rows)
            for c in range(4):
                image[view, 1, c, rows, :] = second[c] + jnp.where(tile_lane < SLOT, rims[c], 0.0)
            return carry

        lax.fori_loop(0, tall // 8, row_body, 0)

    def rim_copies(view):
        rim = RIMS[view]
        top, mid, low = pl.ds(0, rim), pl.ds(rim, LEN), pl.ds(rim + LEN, rim)
        near = pl.ds(0, rim)
        moves = {
            ROW_UP: (image.at[view, :, :, top, :], from_row.at[view, 0, :, :, near, :]),
            ROW_DOWN: (image.at[view, :, :, low, :], from_row.at[view, 1, :, :, near, :]),
            COL_LEFT: (left.at[view, mid, :], from_col.at[view, 0]),
            COL_RIGHT: (right.at[view, mid, :], from_col.at[view, 1]),
            UP_LEFT: (left.at[view, top, :], from_corner.at[view, 0, near, :]),
            UP_RIGHT: (right.at[view, top, :], from_corner.at[view, 1, near, :]),
            DOWN_LEFT: (left.at[view, low, :], from_corner.at[view, 2, near, :]),
            DOWN_RIGHT: (right.at[view, low, :], from_corner.at[view, 3, near, :]),
        }
        return [
            pltpu.make_async_remote_copy(
                src_ref=src, dst_ref=dst,
                send_sem=send_rim.at[view, way], recv_sem=recv_rim.at[view, way],
                device_id=around[way], device_id_type=MESH,
            )
            for way, (src, dst) in moves.items()
        ]

    def fold(view):
        rim = RIMS[view]
        tiles = LEN // 8
        for i in range(tiles):
            rows = slice(rim + i * 8, rim + i * 8 + 8)
            here = slice(i * 8, i * 8 + 8)
            from_right = from_col[view, 0, here, :]
            from_left = from_col[view, 1, here, :]
            above = i * 8 < rim
            below = i * 8 >= LEN - rim
            if above:
                from_right += from_corner[view, 2, here, :]
                from_left += from_corner[view, 3, here, :]
            if below:
                lows = slice(i * 8 - (LEN - rim), i * 8 - (LEN - rim) + 8)
                from_right += from_corner[view, 0, lows, :]
                from_left += from_corner[view, 1, lows, :]
            for c in range(4):
                own = [image[view, b, c, rows, :] for b in range(2)]
                own[0] += jnp.where(
                    tile_lane < SLOT, pltpu.roll(from_left, (-SLOT * c) % LEN, 1), 0.0
                )
                own[1] += jnp.where(
                    tile_lane >= LEN - SLOT,
                    pltpu.roll(from_right, (LEN - SLOT - SLOT * c) % LEN, 1), 0.0,
                )
                for b in range(2):
                    if above:
                        own[b] += from_row[view, 1, b, c, here, :]
                    if below:
                        own[b] += from_row[view, 0, b, c, lows, :]
                    image[view, b, c, rows, :] = own[b]
        for k in range(sections):
            place_of = lax.rem(sign * (k - me) + sections, sections)
            for b in range(2):
                for c in range(4):
                    part = image[
                        view, b, c, pl.ds(rim + k, LEN // sections, stride=sections), :
                    ]
                    sent[view, place_of, b, c] = jnp.exp(-part) if c == 3 else part

    def over(view, near, far):
        mine_first = orders[view, 0] == odd
        weight_near = jnp.where(mine_first, 1.0, far[3])
        weight_far = jnp.where(mine_first, near[3], 1.0)
        return [near[c] * weight_near + far[c] * weight_far for c in range(3)] + [near[3] * far[3]]

    def near_copies(view):
        return [
            pltpu.make_async_remote_copy(
                src_ref=sent.at[view, e], dst_ref=raw.at[view, e - 1],
                send_sem=send_near.at[view, e - 1], recv_sem=recv_near.at[view, e - 1],
                device_id={"depth": partner}, device_id_type=MESH,
            )
            for e in (4, 3, 2, 1)
        ]

    def far_copy(view, e):
        other = lax.rem(me - sign * (sections - e) + 2 * sections, sections)
        slot = lax.rem(me // 2 - other // 2 + sections // 2, sections // 2)
        return pltpu.make_async_remote_copy(
            src_ref=sent.at[view, e], dst_ref=got[view].at[slot],
            send_sem=send_far.at[view, e - 5], recv_sem=recv_far.at[view, slot],
            device_id={"depth": other}, device_id_type=MESH,
        )

    def merge(view):
        for e in (5, 6, 7):
            near_sends[view][e - 5].wait_recv()
            for b in range(2):
                merged = over(
                    view, [sent[view, e, b, c] for c in range(4)], [raw[view, 7 - (e - 1), b, c] for c in range(4)]
                )
                for c in range(4):
                    sent[view, e, b, c] = merged[c]
            far_sends[view].append(far_copy(view, e))
            far_sends[view][-1].start()
        near_sends[view][3].wait_recv()
        for b in range(2):
            merged = over(
                view, [sent[view, 0, b, c] for c in range(4)], [raw[view, 0, b, c] for c in range(4)]
            )
            for c in range(4):
                got[view][0, b, c] = merged[c]

    def composite(view):
        backward = orders[view, 0]
        pairs = sections // 2
        for slot in range(1, pairs):
            pltpu.make_async_remote_copy(
                src_ref=sent.at[view, 5], dst_ref=got[view].at[slot],
                send_sem=send_far.at[view, 0], recv_sem=recv_far.at[view, slot],
                device_id={"depth": partner}, device_id_type=MESH,
            ).wait_recv()
        rows = LEN // sections
        for b in range(2):
            cols = slice(b * LEN, (b + 1) * LEN)
            through = jnp.ones((rows, LEN), jnp.float32)
            colors = [jnp.zeros((rows, LEN), jnp.float32) for _ in range(3)]
            for step in range(pairs):
                pair = step + backward * (pairs - 1 - 2 * step)
                slot = lax.rem(pair - me // 2 + pairs, pairs)
                for c in range(3):
                    colors[c] += got[view][slot, b, c] * through
                through = through * got[view][slot, b, 3]
            for c in range(3):
                out[view, c, :, cols] = colors[c]
            out[view, 3, :, cols] = through

    rim_sends, near_sends, far_sends = [], [], [[] for _ in range(VIEWS)]

    def settle(view):
        for copy in rim_sends[view]:
            copy.wait()
        fold(view)
        near_sends.append(near_copies(view))
        for copy in near_sends[view]:
            copy.start()

    for load in loads:
        load.wait()
    for view in range(VIEWS):
        resample(view)
        if view > 0:
            settle(view - 1)
        shade(view)
        if view == 0:
            pl.semaphore_wait(barrier, 8 + sections - 1)
        rim_sends.append(rim_copies(view))
        for copy in rim_sends[view]:
            copy.start()
    merge(0)
    settle(2)
    merge(1)
    composite(0)
    merge(2)
    composite(1)
    composite(2)
    for view in range(VIEWS):
        for copy in near_sends[view] + far_sends[view]:
            copy.wait_send()


def local(density, emission, offsets, view_order, sections, bands, stripes):
    rows, columns = LEN // sections, 2 * LEN
    vmem, smem, hbm = (
        pl.BlockSpec(memory_space=space) for space in (pltpu.VMEM, pltpu.SMEM, pltpu.HBM)
    )
    image = pl.pallas_call(
        functools.partial(kernel, sections, bands, stripes),
        out_shape=jax.ShapeDtypeStruct((VIEWS, 4, rows, columns), jnp.float32),
        in_specs=[hbm, hbm, smem, smem],
        out_specs=vmem,
        scratch_shapes=[
            pltpu.VMEM(density.shape, density.dtype),
            pltpu.VMEM(emission.shape, emission.dtype),
            pltpu.VMEM((3, SLICES, 4, TALL, LEN), jnp.float32),
            pltpu.VMEM((VIEWS, 2, 4, TALL, LEN), jnp.float32),
            pltpu.VMEM((VIEWS, TALL, LEN), jnp.float32),
            pltpu.VMEM((VIEWS, TALL, LEN), jnp.float32),
            pltpu.VMEM((VIEWS, 2, 2, 4, RIM, LEN), jnp.float32),
            pltpu.VMEM((VIEWS, 2, LEN, LEN), jnp.float32),
            pltpu.VMEM((VIEWS, 4, RIM, LEN), jnp.float32),
            pltpu.VMEM((VIEWS, sections, 2, 4, rows, LEN), jnp.float32),
            pltpu.VMEM((VIEWS, 4, 2, 4, rows, LEN), jnp.float32),
            pltpu.VMEM((sections // 2, 2, 4, rows, LEN), jnp.float32),
            pltpu.VMEM((sections // 2, 2, 4, rows, LEN), jnp.float32),
            pltpu.VMEM((sections // 2, 2, 4, rows, LEN), jnp.float32),
            pltpu.SemaphoreType.DMA((2,)),
            pltpu.SemaphoreType.DMA((VIEWS, 8)),
            pltpu.SemaphoreType.DMA((VIEWS, 8)),
            pltpu.SemaphoreType.DMA((VIEWS, 4)),
            pltpu.SemaphoreType.DMA((VIEWS, 4)),
            pltpu.SemaphoreType.DMA((VIEWS, 4)),
            pltpu.SemaphoreType.DMA((VIEWS, 4)),
        ],
        compiler_params=pltpu.CompilerParams(
            collective_id=0, has_side_effects=True, vmem_limit_bytes=60 * 1024 * 1024
        ),
    )(density, emission, offsets, view_order)
    return image.reshape(VIEWS, 4, rows, 1, columns)


def solution(mesh):
    return jax.shard_map(
        functools.partial(
            local, sections=mesh.shape["depth"], bands=mesh.shape["row"], stripes=mesh.shape["col"]
        ),
        mesh=mesh,
        in_specs=(
            P("depth", "row", "col"),
            P(None, "depth", "row", "col"),
            P(None, None, "depth", "row", "col"),
            P(None, "row"),
        ),
        out_specs=P(None, None, "row", "depth", "col"),
        check_vma=False,
    )
```

```python
import functools

import jax
import jax.numpy as jnp
from jax import lax
from jax.experimental import pallas as pl
from jax.experimental.pallas import tpu as pltpu
from jax.sharding import PartitionSpec as P

MESH = pl.DeviceIdType.MESH
VIEWS = 3
MARGIN = 16
JIT = 8
SLICES = 8
LEN = 128
SHEAR_ROWS = (0.75, -0.5, 0.25)
SHEAR_COLS = (-0.25, 0.625, -0.875)
RIMS = tuple(
    -(-int(abs(a) * (MARGIN - 2) * (SLICES - 1) / SLICES + 1 + JIT) // 8) * 8 for a in SHEAR_ROWS
)
RIM = max(RIMS)
TALL = LEN + 2 * RIM
SLOT = 32

ROW_UP, ROW_DOWN, COL_LEFT, COL_RIGHT, UP_LEFT, UP_RIGHT, DOWN_LEFT, DOWN_RIGHT = range(8)


def shift_of(rate, z):
    return rate * (MARGIN - 2) / SLICES * (2.0 * z - (SLICES - 1))


def tent(distance):
    return jnp.maximum(0.0, 1.0 - jnp.abs(distance)).astype(jnp.bfloat16)


def kernel(
    sections, bands, stripes,
    density_hbm, emission_hbm, offsets, orders, out,
    density, emission, foot, image, left, right,
    from_row, from_col, from_corner, sent, raw, got_0, got_1, got_2,
    load_sem, send_rim, recv_rim, send_near, recv_near, send_far, recv_far,
):
    loads = (
        pltpu.make_async_copy(density_hbm, density, load_sem.at[0]),
        pltpu.make_async_copy(emission_hbm, emission, load_sem.at[1]),
    )
    for load in loads:
        load.start()
    got = (got_0, got_1, got_2)
    me = lax.axis_index("depth")
    odd = lax.rem(me, 2)
    sign = 1 - 2 * odd
    partner = me + sign
    band = lax.axis_index("row")
    stripe = lax.axis_index("col")

    def place(drow, dcol):
        return {
            "row": lax.rem(band + drow + bands, bands),
            "col": lax.rem(stripe + dcol + stripes, stripes),
        }

    around = {
        ROW_UP: place(-1, 0), ROW_DOWN: place(1, 0), COL_LEFT: place(0, -1), COL_RIGHT: place(0, 1),
        UP_LEFT: place(-1, -1), UP_RIGHT: place(-1, 1), DOWN_LEFT: place(1, -1), DOWN_RIGHT: place(1, 1),
    }
    barrier = pltpu.get_barrier_semaphore()
    for device in around.values():
        pl.semaphore_signal(barrier, inc=1, device_id=device, device_id_type=MESH)
    for hop in range(1, sections):
        pl.semaphore_signal(
            barrier, inc=1, device_id={"depth": lax.rem(me + hop, sections)}, device_id_type=MESH
        )

    lane = lax.broadcasted_iota(jnp.int32, (LEN, 2 * LEN), 1)
    cell = lax.broadcasted_iota(jnp.int32, (LEN, 2 * LEN), 0)
    tail = lane - LEN
    nowhere = -4096
    column = (
        jnp.where(lane < LEN, lane, jnp.where(tail < SLOT, tail + LEN,
                  jnp.where(tail < 2 * SLOT, tail - 2 * SLOT, nowhere))),
        jnp.where(lane < LEN, lane, jnp.where(tail < 2 * SLOT, nowhere,
                  jnp.where(tail < 3 * SLOT, tail + LEN - 2 * SLOT, tail - LEN))),
    )
    col_base = [(c - cell).astype(jnp.float32) for c in column]
    tile_lane = lax.broadcasted_iota(jnp.int32, (8, LEN), 1)

    def resample(view):
        rim = RIMS[view]
        tall = LEN + 2 * rim
        row_base = (
            lax.broadcasted_iota(jnp.int32, (tall, LEN), 0) - rim
            - lax.broadcasted_iota(jnp.int32, (tall, LEN), 1)
        ).astype(jnp.float32)

        def slice_body(z, carry):
            zf = z.astype(jnp.float32)
            owns, tails, row_weights = [], [], []
            for b in range(2):
                oy = offsets[0, b, view].astype(jnp.float32)
                ox = offsets[1, b, view].astype(jnp.float32)
                cols = slice(b * LEN, (b + 1) * LEN)
                cells = jnp.concatenate(
                    [density[z, :, cols]] + [emission[c, z, :, cols] for c in range(3)], 0
                )
                col_weights = tent(col_base[b] - (ox + shift_of(SHEAR_COLS[view], zf)))
                lines = jnp.dot(
                    cells, col_weights, preferred_element_type=jnp.float32
                ).astype(jnp.bfloat16)
                row_weights.append(tent(row_base - (oy + shift_of(SHEAR_ROWS[view], zf))))
                owns.append([lines[f * LEN:(f + 1) * LEN, :LEN] for f in range(4)])
                tails.append([lines[f * LEN:(f + 1) * LEN, LEN:] for f in range(4)])
            none = jnp.zeros((LEN, 4 * LEN), jnp.bfloat16)
            above = jnp.concatenate(owns[0] + [none] + tails[0], 1)
            below = jnp.concatenate([none] + owns[1] + tails[1], 1)
            prints = jnp.dot(
                jnp.concatenate(row_weights, 1), jnp.concatenate([above, below], 0),
                preferred_element_type=jnp.float32,
            )
            for region in range(3):
                for f in range(4):
                    at = (region * 4 + f) * LEN
                    foot[region, z, f, 0:tall, :] = prints[:, at:at + LEN]
            return carry

        lax.fori_loop(0, SLICES, slice_body, 0, unroll=8)

    def shade(view):
        rim = RIMS[view]
        tall = LEN + 2 * rim
        backward = orders[view]
        steps = [z + backward * (SLICES - 1 - 2 * z) for z in range(SLICES)]

        def integrate(region, rows):
            through = jnp.ones((8, LEN), jnp.float32)
            depth = jnp.zeros((8, LEN), jnp.float32)
            colors = [jnp.zeros((8, LEN), jnp.float32) for _ in range(3)]
            for z in steps:
                e = foot[region, z, 0, rows, :]
                after = through * jnp.exp(-e)
                weight = through - after
                through = after
                depth += e
                for c in range(3):
                    colors[c] += foot[region, z, 1 + c, rows, :] * weight
            return colors + [depth]

        def row_body(i, carry):
            rows = pl.ds(pl.multiple_of(i * 8, 8), 8)
            rims = integrate(2, rows)
            lefts = jnp.zeros((8, LEN), jnp.float32)
            rights = jnp.zeros((8, LEN), jnp.float32)
            for c in range(4):
                mine = jnp.where((tile_lane >= SLOT) & (tile_lane < 2 * SLOT), rims[c], 0.0)
                lefts += pltpu.roll(mine, (SLOT * c - SLOT) % LEN, 1)
                mine = jnp.where((tile_lane >= 2 * SLOT) & (tile_lane < 3 * SLOT), rims[c], 0.0)
                rights += pltpu.roll(mine, (SLOT * c - 2 * SLOT) % LEN, 1)
            left[view, rows, :] = lefts
            right[view, rows, :] = rights
            first = integrate(0, rows)
            for c in range(4):
                image[view, 0, c, rows, :] = first[c] + jnp.where(tile_lane >= 3 * SLOT, rims[c], 0.0)
            second = integrate(1, rows)
            for c in range(4):
                image[view, 1, c, rows, :] = second[c] + jnp.where(tile_lane < SLOT, rims[c], 0.0)
            return carry

        lax.fori_loop(0, tall // 8, row_body, 0)

    def rim_copies(view):
        rim = RIMS[view]
        top, mid, low = pl.ds(0, rim), pl.ds(rim, LEN), pl.ds(rim + LEN, rim)
        near = pl.ds(0, rim)
        moves = {
            ROW_UP: (image.at[view, :, :, top, :], from_row.at[view, 0, :, :, near, :]),
            ROW_DOWN: (image.at[view, :, :, low, :], from_row.at[view, 1, :, :, near, :]),
            COL_LEFT: (left.at[view, mid, :], from_col.at[view, 0]),
            COL_RIGHT: (right.at[view, mid, :], from_col.at[view, 1]),
            UP_LEFT: (left.at[view, top, :], from_corner.at[view, 0, near, :]),
            UP_RIGHT: (right.at[view, top, :], from_corner.at[view, 1, near, :]),
            DOWN_LEFT: (left.at[view, low, :], from_corner.at[view, 2, near, :]),
            DOWN_RIGHT: (right.at[view, low, :], from_corner.at[view, 3, near, :]),
        }
        return [
            pltpu.make_async_remote_copy(
                src_ref=src, dst_ref=dst,
                send_sem=send_rim.at[view, way], recv_sem=recv_rim.at[view, way],
                device_id=around[way], device_id_type=MESH,
            )
            for way, (src, dst) in moves.items()
        ]

    def fold(view):
        rim = RIMS[view]
        tiles = LEN // 8
        for i in range(tiles):
            rows = slice(rim + i * 8, rim + i * 8 + 8)
            here = slice(i * 8, i * 8 + 8)
            from_right = from_col[view, 0, here, :]
            from_left = from_col[view, 1, here, :]
            above = i * 8 < rim
            below = i * 8 >= LEN - rim
            if above:
                from_right += from_corner[view, 2, here, :]
                from_left += from_corner[view, 3, here, :]
            if below:
                lows = slice(i * 8 - (LEN - rim), i * 8 - (LEN - rim) + 8)
                from_right += from_corner[view, 0, lows, :]
                from_left += from_corner[view, 1, lows, :]
            for c in range(4):
                own = [image[view, b, c, rows, :] for b in range(2)]
                own[0] += jnp.where(
                    tile_lane < SLOT, pltpu.roll(from_left, (-SLOT * c) % LEN, 1), 0.0
                )
                own[1] += jnp.where(
                    tile_lane >= LEN - SLOT,
                    pltpu.roll(from_right, (LEN - SLOT - SLOT * c) % LEN, 1), 0.0,
                )
                for b in range(2):
                    if above:
                        own[b] += from_row[view, 1, b, c, here, :]
                    if below:
                        own[b] += from_row[view, 0, b, c, lows, :]
                    image[view, b, c, rows, :] = own[b]
        for k in range(sections):
            place_of = lax.rem(sign * (k - me) + sections, sections)
            for b in range(2):
                for c in range(4):
                    part = image[
                        view, b, c, pl.ds(rim + k, LEN // sections, stride=sections), :
                    ]
                    sent[view, place_of, b, c] = jnp.exp(-part) if c == 3 else part

    def over(view, near, far):
        mine_first = orders[view] == odd
        weight_near = jnp.where(mine_first, 1.0, far[3])
        weight_far = jnp.where(mine_first, near[3], 1.0)
        return [near[c] * weight_near + far[c] * weight_far for c in range(3)] + [near[3] * far[3]]

    def near_copies(view):
        return [
            pltpu.make_async_remote_copy(
                src_ref=sent.at[view, e], dst_ref=raw.at[view, e - 1],
                send_sem=send_near.at[view, e - 1], recv_sem=recv_near.at[view, e - 1],
                device_id={"depth": partner}, device_id_type=MESH,
            )
            for e in (4, 3, 2, 1)
        ]

    def far_copy(view, e):
        other = lax.rem(me - sign * (sections - e) + 2 * sections, sections)
        slot = lax.rem(me // 2 - other // 2 + sections // 2, sections // 2)
        return pltpu.make_async_remote_copy(
            src_ref=sent.at[view, e], dst_ref=got[view].at[slot],
            send_sem=send_far.at[view, e - 5], recv_sem=recv_far.at[view, slot],
            device_id={"depth": other}, device_id_type=MESH,
        )

    def merge(view):
        for e in (5, 6, 7):
            near_sends[view][e - 5].wait_recv()
            for b in range(2):
                merged = over(
                    view, [sent[view, e, b, c] for c in range(4)], [raw[view, 7 - (e - 1), b, c] for c in range(4)]
                )
                for c in range(4):
                    sent[view, e, b, c] = merged[c]
            far_sends[view].append(far_copy(view, e))
            far_sends[view][-1].start()
        near_sends[view][3].wait_recv()
        for b in range(2):
            merged = over(
                view, [sent[view, 0, b, c] for c in range(4)], [raw[view, 0, b, c] for c in range(4)]
            )
            for c in range(4):
                got[view][0, b, c] = merged[c]

    def composite(view):
        backward = orders[view]
        pairs = sections // 2
        for slot in range(1, pairs):
            pltpu.make_async_remote_copy(
                src_ref=sent.at[view, 5], dst_ref=got[view].at[slot],
                send_sem=send_far.at[view, 0], recv_sem=recv_far.at[view, slot],
                device_id={"depth": partner}, device_id_type=MESH,
            ).wait_recv()
        rows = LEN // sections
        for b in range(2):
            lines = pl.ds(b, rows, stride=2)
            through = jnp.ones((rows, LEN), jnp.float32)
            colors = [jnp.zeros((rows, LEN), jnp.float32) for _ in range(3)]
            for step in range(pairs):
                pair = step + backward * (pairs - 1 - 2 * step)
                slot = lax.rem(pair - me // 2 + pairs, pairs)
                for c in range(3):
                    colors[c] += got[view][slot, b, c] * through
                through = through * got[view][slot, b, 3]
            for c in range(3):
                out[view, c, lines, :] = colors[c]
            out[view, 3, lines, :] = through

    rim_sends, near_sends, far_sends = [], [], [[] for _ in range(VIEWS)]

    def settle(view):
        for copy in rim_sends[view]:
            copy.wait()
        fold(view)
        near_sends.append(near_copies(view))
        for copy in near_sends[view]:
            copy.start()

    for load in loads:
        load.wait()
    def render(view):
        resample(view)
        shade(view)
        if view == 0:
            pl.semaphore_wait(barrier, 8 + sections - 1)
        rim_sends.append(rim_copies(view))
        for copy in rim_sends[view]:
            copy.start()

    render(0)
    render(1)
    settle(0)
    render(2)
    settle(1)
    merge(0)
    settle(2)
    merge(1)
    composite(0)
    merge(2)
    composite(1)
    composite(2)
    for view in range(VIEWS):
        for copy in near_sends[view] + far_sends[view]:
            copy.wait_send()


def local(density, emission, offsets, view_order, sections, bands, stripes):
    rows, columns = LEN // sections, 2 * LEN
    vmem, smem, hbm = (
        pl.BlockSpec(memory_space=space) for space in (pltpu.VMEM, pltpu.SMEM, pltpu.HBM)
    )
    image = pl.pallas_call(
        functools.partial(kernel, sections, bands, stripes),
        out_shape=jax.ShapeDtypeStruct((VIEWS, 4, 2 * rows, LEN), jnp.float32),
        in_specs=[hbm, hbm, smem, smem],
        out_specs=vmem,
        scratch_shapes=[
            pltpu.VMEM(density.shape, density.dtype),
            pltpu.VMEM(emission.shape, emission.dtype),
            pltpu.VMEM((3, SLICES, 4, TALL, LEN), jnp.float32),
            pltpu.VMEM((VIEWS, 2, 4, TALL, LEN), jnp.float32),
            pltpu.VMEM((VIEWS, TALL, LEN), jnp.float32),
            pltpu.VMEM((VIEWS, TALL, LEN), jnp.float32),
            pltpu.VMEM((VIEWS, 2, 2, 4, RIM, LEN), jnp.float32),
            pltpu.VMEM((VIEWS, 2, LEN, LEN), jnp.float32),
            pltpu.VMEM((VIEWS, 4, RIM, LEN), jnp.float32),
            pltpu.VMEM((VIEWS, sections, 2, 4, rows, LEN), jnp.float32),
            pltpu.VMEM((VIEWS, 4, 2, 4, rows, LEN), jnp.float32),
            pltpu.VMEM((sections // 2, 2, 4, rows, LEN), jnp.float32),
            pltpu.VMEM((sections // 2, 2, 4, rows, LEN), jnp.float32),
            pltpu.VMEM((sections // 2, 2, 4, rows, LEN), jnp.float32),
            pltpu.SemaphoreType.DMA((2,)),
            pltpu.SemaphoreType.DMA((VIEWS, 8)),
            pltpu.SemaphoreType.DMA((VIEWS, 8)),
            pltpu.SemaphoreType.DMA((VIEWS, 4)),
            pltpu.SemaphoreType.DMA((VIEWS, 4)),
            pltpu.SemaphoreType.DMA((VIEWS, 4)),
            pltpu.SemaphoreType.DMA((VIEWS, 4)),
        ],
        compiler_params=pltpu.CompilerParams(
            collective_id=0, has_side_effects=True, vmem_limit_bytes=60 * 1024 * 1024
        ),
    )(
        density, emission,
        offsets.transpose(1, 2, 3, 4, 0).reshape(2, 2, VIEWS), view_order.reshape(-1),
    )
    return image.reshape(VIEWS, 4, rows, 1, columns)


def solution(mesh):
    return jax.shard_map(
        functools.partial(
            local, sections=mesh.shape["depth"], bands=mesh.shape["row"], stripes=mesh.shape["col"]
        ),
        mesh=mesh,
        in_specs=(
            P("depth", "row", "col"),
            P(None, "depth", "row", "col"),
            P(None, None, "depth", "row", "col"),
            P(None, "row"),
        ),
        out_specs=P(None, None, "row", "depth", "col"),
        check_vma=False,
    )
```

```python
import functools

import jax
import jax.numpy as jnp
from jax import lax
from jax.experimental import pallas as pl
from jax.experimental.pallas import tpu as pltpu
from jax.sharding import PartitionSpec as P

MESH = pl.DeviceIdType.MESH
VIEWS = 3
MARGIN = 16
JIT = 8
SLICES = 8
LEN = 128
SHEAR_ROWS = (0.75, -0.5, 0.25)
SHEAR_COLS = (-0.25, 0.625, -0.875)
RIMS = tuple(
    -(-int(abs(a) * (MARGIN - 2) * (SLICES - 1) / SLICES + 1 + JIT) // 8) * 8 for a in SHEAR_ROWS
)
RIM = max(RIMS)
TALL = LEN + 2 * RIM
SLOT = 32

ROW_UP, ROW_DOWN, COL_LEFT, COL_RIGHT, UP_LEFT, UP_RIGHT, DOWN_LEFT, DOWN_RIGHT = range(8)


def shift_of(rate, z):
    return rate * (MARGIN - 2) / SLICES * (2.0 * z - (SLICES - 1))


def tent(distance):
    return jnp.maximum(0.0, 1.0 - jnp.abs(distance)).astype(jnp.bfloat16)


def kernel(
    sections, bands, stripes,
    density_hbm, emission_hbm, offsets, orders, out,
    density, emission, foot, image, left, right,
    from_row, from_col, from_corner, sent, raw, got_0, got_1, got_2,
    load_sem, send_rim, recv_rim, send_near, recv_near, send_far, recv_far,
):
    loads = (
        pltpu.make_async_copy(density_hbm, density, load_sem.at[0]),
        pltpu.make_async_copy(emission_hbm, emission, load_sem.at[1]),
    )
    for load in loads:
        load.start()
    got = (got_0, got_1, got_2)
    me = lax.axis_index("depth")
    odd = lax.rem(me, 2)
    sign = 1 - 2 * odd
    partner = me + sign
    band = lax.axis_index("row")
    stripe = lax.axis_index("col")

    def place(drow, dcol):
        return {
            "row": lax.rem(band + drow + bands, bands),
            "col": lax.rem(stripe + dcol + stripes, stripes),
        }

    around = {
        ROW_UP: place(-1, 0), ROW_DOWN: place(1, 0), COL_LEFT: place(0, -1), COL_RIGHT: place(0, 1),
        UP_LEFT: place(-1, -1), UP_RIGHT: place(-1, 1), DOWN_LEFT: place(1, -1), DOWN_RIGHT: place(1, 1),
    }
    barrier = pltpu.get_barrier_semaphore()
    for device in around.values():
        pl.semaphore_signal(barrier, inc=1, device_id=device, device_id_type=MESH)
    for hop in range(1, sections):
        pl.semaphore_signal(
            barrier, inc=1, device_id={"depth": lax.rem(me + hop, sections)}, device_id_type=MESH
        )

    lane = lax.broadcasted_iota(jnp.int32, (LEN, 2 * LEN), 1)
    cell = lax.broadcasted_iota(jnp.int32, (LEN, 2 * LEN), 0)
    tail = lane - LEN
    nowhere = -4096
    column = (
        jnp.where(lane < LEN, lane, jnp.where(tail < SLOT, tail + LEN,
                  jnp.where(tail < 2 * SLOT, tail - 2 * SLOT, nowhere))),
        jnp.where(lane < LEN, lane, jnp.where(tail < 2 * SLOT, nowhere,
                  jnp.where(tail < 3 * SLOT, tail + LEN - 2 * SLOT, tail - LEN))),
    )
    col_base = [(c - cell).astype(jnp.float32) for c in column]
    tile_lane = lax.broadcasted_iota(jnp.int32, (8, LEN), 1)

    def resample(view):
        rim = RIMS[view]
        tall = LEN + 2 * rim
        row_base = (
            lax.broadcasted_iota(jnp.int32, (tall, LEN), 0) - rim
            - lax.broadcasted_iota(jnp.int32, (tall, LEN), 1)
        ).astype(jnp.float32)

        def slice_body(z, carry):
            zf = z.astype(jnp.float32)
            owns, tails, row_weights = [], [], []
            for b in range(2):
                oy = offsets[0, b, view].astype(jnp.float32)
                ox = offsets[1, b, view].astype(jnp.float32)
                cols = slice(b * LEN, (b + 1) * LEN)
                cells = jnp.concatenate(
                    [density[z, :, cols]] + [emission[c, z, :, cols] for c in range(3)], 0
                )
                col_weights = tent(col_base[b] - (ox + shift_of(SHEAR_COLS[view], zf)))
                lines = jnp.dot(
                    cells, col_weights, preferred_element_type=jnp.float32
                ).astype(jnp.bfloat16)
                row_weights.append(tent(row_base - (oy + shift_of(SHEAR_ROWS[view], zf))))
                owns.append([lines[f * LEN:(f + 1) * LEN, :LEN] for f in range(4)])
                tails.append([lines[f * LEN:(f + 1) * LEN, LEN:] for f in range(4)])
            none = jnp.zeros((LEN, 4 * LEN), jnp.bfloat16)
            above = jnp.concatenate(owns[0] + [none] + tails[0], 1)
            below = jnp.concatenate([none] + owns[1] + tails[1], 1)
            prints = jnp.dot(
                jnp.concatenate(row_weights, 1), jnp.concatenate([above, below], 0),
                preferred_element_type=jnp.float32,
            )
            for region in range(3):
                for f in range(4):
                    at = (region * 4 + f) * LEN
                    foot[region, z, f, 0:tall, :] = prints[:, at:at + LEN]
            return carry

        lax.fori_loop(0, SLICES, slice_body, 0, unroll=8)

    def shade(view):
        rim = RIMS[view]
        tall = LEN + 2 * rim
        backward = orders[view]
        steps = [z + backward * (SLICES - 1 - 2 * z) for z in range(SLICES)]

        def integrate(region, rows):
            through = jnp.ones((8, LEN), jnp.float32)
            depth = jnp.zeros((8, LEN), jnp.float32)
            colors = [jnp.zeros((8, LEN), jnp.float32) for _ in range(3)]
            for z in steps:
                e = foot[region, z, 0, rows, :]
                after = through * jnp.exp(-e)
                weight = through - after
                through = after
                depth += e
                for c in range(3):
                    colors[c] += foot[region, z, 1 + c, rows, :] * weight
            return colors + [depth]

        def row_body(i, carry):
            rows = pl.ds(pl.multiple_of(i * 8, 8), 8)
            rims = integrate(2, rows)
            lefts = jnp.zeros((8, LEN), jnp.float32)
            rights = jnp.zeros((8, LEN), jnp.float32)
            for c in range(4):
                mine = jnp.where((tile_lane >= SLOT) & (tile_lane < 2 * SLOT), rims[c], 0.0)
                lefts += pltpu.roll(mine, (SLOT * c - SLOT) % LEN, 1)
                mine = jnp.where((tile_lane >= 2 * SLOT) & (tile_lane < 3 * SLOT), rims[c], 0.0)
                rights += pltpu.roll(mine, (SLOT * c - 2 * SLOT) % LEN, 1)
            left[view, rows, :] = lefts
            right[view, rows, :] = rights
            first = integrate(0, rows)
            for c in range(4):
                image[view, 0, c, rows, :] = first[c] + jnp.where(tile_lane >= 3 * SLOT, rims[c], 0.0)
            second = integrate(1, rows)
            for c in range(4):
                image[view, 1, c, rows, :] = second[c] + jnp.where(tile_lane < SLOT, rims[c], 0.0)
            return carry

        lax.fori_loop(0, tall // 8, row_body, 0)

    def rim_copies(view):
        rim = RIMS[view]
        top, mid, low = pl.ds(0, rim), pl.ds(rim, LEN), pl.ds(rim + LEN, rim)
        near = pl.ds(0, rim)
        moves = {
            UP_LEFT: (left.at[view, top, :], from_corner.at[view, 0, near, :]),
            UP_RIGHT: (right.at[view, top, :], from_corner.at[view, 1, near, :]),
            DOWN_LEFT: (left.at[view, low, :], from_corner.at[view, 2, near, :]),
            DOWN_RIGHT: (right.at[view, low, :], from_corner.at[view, 3, near, :]),
            ROW_UP: (image.at[view, :, :, top, :], from_row.at[view, 0, :, :, near, :]),
            ROW_DOWN: (image.at[view, :, :, low, :], from_row.at[view, 1, :, :, near, :]),
            COL_LEFT: (left.at[view, mid, :], from_col.at[view, 0]),
            COL_RIGHT: (right.at[view, mid, :], from_col.at[view, 1]),
        }
        return [
            pltpu.make_async_remote_copy(
                src_ref=src, dst_ref=dst,
                send_sem=send_rim.at[view, way], recv_sem=recv_rim.at[view, way],
                device_id=around[way], device_id_type=MESH,
            )
            for way, (src, dst) in moves.items()
        ]

    def fold(view):
        rim = RIMS[view]
        tiles = LEN // 8
        for i in range(tiles):
            rows = slice(rim + i * 8, rim + i * 8 + 8)
            here = slice(i * 8, i * 8 + 8)
            from_right = from_col[view, 0, here, :]
            from_left = from_col[view, 1, here, :]
            above = i * 8 < rim
            below = i * 8 >= LEN - rim
            if above:
                from_right += from_corner[view, 2, here, :]
                from_left += from_corner[view, 3, here, :]
            if below:
                lows = slice(i * 8 - (LEN - rim), i * 8 - (LEN - rim) + 8)
                from_right += from_corner[view, 0, lows, :]
                from_left += from_corner[view, 1, lows, :]
            for c in range(4):
                own = [image[view, b, c, rows, :] for b in range(2)]
                own[0] += jnp.where(
                    tile_lane < SLOT, pltpu.roll(from_left, (-SLOT * c) % LEN, 1), 0.0
                )
                own[1] += jnp.where(
                    tile_lane >= LEN - SLOT,
                    pltpu.roll(from_right, (LEN - SLOT - SLOT * c) % LEN, 1), 0.0,
                )
                for b in range(2):
                    if above:
                        own[b] += from_row[view, 1, b, c, here, :]
                    if below:
                        own[b] += from_row[view, 0, b, c, lows, :]
                    image[view, b, c, rows, :] = own[b]
        for k in range(sections):
            place_of = lax.rem(sign * (k - me) + sections, sections)
            for b in range(2):
                for c in range(4):
                    part = image[
                        view, b, c, pl.ds(rim + k, LEN // sections, stride=sections), :
                    ]
                    sent[view, place_of, b, c] = jnp.exp(-part) if c == 3 else part

    def over(view, near, far):
        mine_first = orders[view] == odd
        weight_near = jnp.where(mine_first, 1.0, far[3])
        weight_far = jnp.where(mine_first, near[3], 1.0)
        return [near[c] * weight_near + far[c] * weight_far for c in range(3)] + [near[3] * far[3]]

    def near_copies(view):
        return [
            pltpu.make_async_remote_copy(
                src_ref=sent.at[view, e], dst_ref=raw.at[view, e - 1],
                send_sem=send_near.at[view, e - 1], recv_sem=recv_near.at[view, e - 1],
                device_id={"depth": partner}, device_id_type=MESH,
            )
            for e in (4, 3, 2, 1)
        ]

    def far_copy(view, e):
        other = lax.rem(me - sign * (sections - e) + 2 * sections, sections)
        slot = lax.rem(me // 2 - other // 2 + sections // 2, sections // 2)
        return pltpu.make_async_remote_copy(
            src_ref=sent.at[view, e], dst_ref=got[view].at[slot],
            send_sem=send_far.at[view, e - 5], recv_sem=recv_far.at[view, slot],
            device_id={"depth": other}, device_id_type=MESH,
        )

    def merge(view):
        for e in (5, 6, 7):
            near_sends[view][e - 5].wait_recv()
            for b in range(2):
                merged = over(
                    view, [sent[view, e, b, c] for c in range(4)], [raw[view, 7 - (e - 1), b, c] for c in range(4)]
                )
                for c in range(4):
                    sent[view, e, b, c] = merged[c]
            far_sends[view].append(far_copy(view, e))
            far_sends[view][-1].start()
        near_sends[view][3].wait_recv()
        for b in range(2):
            merged = over(
                view, [sent[view, 0, b, c] for c in range(4)], [raw[view, 0, b, c] for c in range(4)]
            )
            for c in range(4):
                got[view][0, b, c] = merged[c]

    def composite(view):
        backward = orders[view]
        pairs = sections // 2
        for slot in range(1, pairs):
            pltpu.make_async_remote_copy(
                src_ref=sent.at[view, 5], dst_ref=got[view].at[slot],
                send_sem=send_far.at[view, 0], recv_sem=recv_far.at[view, slot],
                device_id={"depth": partner}, device_id_type=MESH,
            ).wait_recv()
        rows = LEN // sections
        for b in range(2):
            lines = pl.ds(b, rows, stride=2)
            through = jnp.ones((rows, LEN), jnp.float32)
            colors = [jnp.zeros((rows, LEN), jnp.float32) for _ in range(3)]
            for step in range(pairs):
                pair = step + backward * (pairs - 1 - 2 * step)
                slot = lax.rem(pair - me // 2 + pairs, pairs)
                for c in range(3):
                    colors[c] += got[view][slot, b, c] * through
                through = through * got[view][slot, b, 3]
            for c in range(3):
                out[view, c, lines, :] = colors[c]
            out[view, 3, lines, :] = through

    rim_sends, near_sends, far_sends = {}, {}, [[] for _ in range(VIEWS)]

    def settle(view):
        for copy in rim_sends[view]:
            copy.wait()
        fold(view)
        near_sends[view] = near_copies(view)
        for copy in near_sends[view]:
            copy.start()

    for load in loads:
        load.wait()
    def render(view):
        resample(view)
        shade(view)
        if view == 2:
            pl.semaphore_wait(barrier, 8 + sections - 1)
        rim_sends[view] = rim_copies(view)
        for copy in rim_sends[view]:
            copy.start()

    render(2)
    render(1)
    settle(2)
    render(0)
    settle(1)
    merge(2)
    settle(0)
    merge(1)
    composite(2)
    merge(0)
    composite(1)
    composite(0)
    for view in range(VIEWS):
        for copy in near_sends[view] + far_sends[view]:
            copy.wait_send()


def local(density, emission, offsets, view_order, sections, bands, stripes):
    rows, columns = LEN // sections, 2 * LEN
    vmem, smem, hbm = (
        pl.BlockSpec(memory_space=space) for space in (pltpu.VMEM, pltpu.SMEM, pltpu.HBM)
    )
    image = pl.pallas_call(
        functools.partial(kernel, sections, bands, stripes),
        out_shape=jax.ShapeDtypeStruct((VIEWS, 4, 2 * rows, LEN), jnp.float32),
        in_specs=[hbm, hbm, smem, smem],
        out_specs=vmem,
        scratch_shapes=[
            pltpu.VMEM(density.shape, density.dtype),
            pltpu.VMEM(emission.shape, emission.dtype),
            pltpu.VMEM((3, SLICES, 4, TALL, LEN), jnp.float32),
            pltpu.VMEM((VIEWS, 2, 4, TALL, LEN), jnp.float32),
            pltpu.VMEM((VIEWS, TALL, LEN), jnp.float32),
            pltpu.VMEM((VIEWS, TALL, LEN), jnp.float32),
            pltpu.VMEM((VIEWS, 2, 2, 4, RIM, LEN), jnp.float32),
            pltpu.VMEM((VIEWS, 2, LEN, LEN), jnp.float32),
            pltpu.VMEM((VIEWS, 4, RIM, LEN), jnp.float32),
            pltpu.VMEM((VIEWS, sections, 2, 4, rows, LEN), jnp.float32),
            pltpu.VMEM((VIEWS, 4, 2, 4, rows, LEN), jnp.float32),
            pltpu.VMEM((sections // 2, 2, 4, rows, LEN), jnp.float32),
            pltpu.VMEM((sections // 2, 2, 4, rows, LEN), jnp.float32),
            pltpu.VMEM((sections // 2, 2, 4, rows, LEN), jnp.float32),
            pltpu.SemaphoreType.DMA((2,)),
            pltpu.SemaphoreType.DMA((VIEWS, 8)),
            pltpu.SemaphoreType.DMA((VIEWS, 8)),
            pltpu.SemaphoreType.DMA((VIEWS, 4)),
            pltpu.SemaphoreType.DMA((VIEWS, 4)),
            pltpu.SemaphoreType.DMA((VIEWS, 4)),
            pltpu.SemaphoreType.DMA((VIEWS, 4)),
        ],
        compiler_params=pltpu.CompilerParams(
            collective_id=0, has_side_effects=True, vmem_limit_bytes=60 * 1024 * 1024
        ),
    )(
        density, emission,
        offsets.transpose(1, 2, 3, 4, 0).reshape(2, 2, VIEWS), view_order.reshape(-1),
    )
    return image.reshape(VIEWS, 4, rows, 1, columns)


def solution(mesh):
    return jax.shard_map(
        functools.partial(
            local, sections=mesh.shape["depth"], bands=mesh.shape["row"], stripes=mesh.shape["col"]
        ),
        mesh=mesh,
        in_specs=(
            P("depth", "row", "col"),
            P(None, "depth", "row", "col"),
            P(None, None, "depth", "row", "col"),
            P(None, "row"),
        ),
        out_specs=P(None, None, "row", "depth", "col"),
        check_vma=False,
    )
```

```python
import functools

import jax
import jax.numpy as jnp
from jax import lax
from jax.experimental import pallas as pl
from jax.experimental.pallas import tpu as pltpu
from jax.sharding import PartitionSpec as P

MESH = pl.DeviceIdType.MESH
VIEWS = 3
MARGIN = 16
JIT = 8
SLICES = 8
LEN = 128
SHEAR_ROWS = (0.75, -0.5, 0.25)
SHEAR_COLS = (-0.25, 0.625, -0.875)
RIMS = tuple(
    -(-int(abs(a) * (MARGIN - 2) * (SLICES - 1) / SLICES + 1 + JIT) // 8) * 8 for a in SHEAR_ROWS
)
RIM = max(RIMS)
TALL = LEN + 2 * RIM
SLOT = 32

ROW_UP, ROW_DOWN, COL_LEFT, COL_RIGHT, UP_LEFT, UP_RIGHT, DOWN_LEFT, DOWN_RIGHT = range(8)


def shift_of(rate, z):
    return rate * (MARGIN - 2) / SLICES * (2.0 * z - (SLICES - 1))


def tent(distance):
    return jnp.maximum(0.0, 1.0 - jnp.abs(distance)).astype(jnp.bfloat16)


def kernel(
    sections, bands, stripes,
    density_hbm, emission_hbm, offsets, orders, out,
    density, emission, foot, image, left, right,
    from_row, from_col, from_corner, sent, raw, got_0, got_1, got_2,
    load_sem, send_rim, recv_rim, send_near, recv_near, send_far, recv_far,
):
    loads = (
        pltpu.make_async_copy(density_hbm, density, load_sem.at[0]),
        pltpu.make_async_copy(emission_hbm, emission, load_sem.at[1]),
    )
    for load in loads:
        load.start()
    got = (got_0, got_1, got_2)
    me = lax.axis_index("depth")
    odd = lax.rem(me, 2)
    sign = 1 - 2 * odd
    partner = me + sign
    band = lax.axis_index("row")
    stripe = lax.axis_index("col")

    def place(drow, dcol):
        return {
            "row": lax.rem(band + drow + bands, bands),
            "col": lax.rem(stripe + dcol + stripes, stripes),
        }

    around = {
        ROW_UP: place(-1, 0), ROW_DOWN: place(1, 0), COL_LEFT: place(0, -1), COL_RIGHT: place(0, 1),
        UP_LEFT: place(-1, -1), UP_RIGHT: place(-1, 1), DOWN_LEFT: place(1, -1), DOWN_RIGHT: place(1, 1),
    }
    barrier = pltpu.get_barrier_semaphore()
    for device in around.values():
        pl.semaphore_signal(barrier, inc=1, device_id=device, device_id_type=MESH)
    for hop in range(1, sections):
        pl.semaphore_signal(
            barrier, inc=1, device_id={"depth": lax.rem(me + hop, sections)}, device_id_type=MESH
        )

    lane = lax.broadcasted_iota(jnp.int32, (LEN, 2 * LEN), 1)
    cell = lax.broadcasted_iota(jnp.int32, (LEN, 2 * LEN), 0)
    tail = lane - LEN
    nowhere = -4096
    column = (
        jnp.where(lane < LEN, lane, jnp.where(tail < SLOT, tail + LEN,
                  jnp.where(tail < 2 * SLOT, tail - 2 * SLOT, nowhere))),
        jnp.where(lane < LEN, lane, jnp.where(tail < 2 * SLOT, nowhere,
                  jnp.where(tail < 3 * SLOT, tail + LEN - 2 * SLOT, tail - LEN))),
    )
    col_base = [(c - cell).astype(jnp.float32) for c in column]
    tile_lane = lax.broadcasted_iota(jnp.int32, (8, LEN), 1)

    def resample(view):
        rim = RIMS[view]
        tall = LEN + 2 * rim
        row_base = (
            lax.broadcasted_iota(jnp.int32, (tall, LEN), 0) - rim
            - lax.broadcasted_iota(jnp.int32, (tall, LEN), 1)
        ).astype(jnp.float32)

        def slice_body(z, carry):
            zf = z.astype(jnp.float32)
            owns, tails, row_weights = [], [], []
            for b in range(2):
                oy = offsets[0, b, view].astype(jnp.float32)
                ox = offsets[1, b, view].astype(jnp.float32)
                cols = slice(b * LEN, (b + 1) * LEN)
                cells = jnp.concatenate(
                    [density[z, :, cols]] + [emission[c, z, :, cols] for c in range(3)], 0
                )
                col_weights = tent(col_base[b] - (ox + shift_of(SHEAR_COLS[view], zf)))
                lines = jnp.dot(
                    cells, col_weights, preferred_element_type=jnp.float32
                ).astype(jnp.bfloat16)
                row_weights.append(tent(row_base - (oy + shift_of(SHEAR_ROWS[view], zf))))
                owns.append([lines[f * LEN:(f + 1) * LEN, :LEN] for f in range(4)])
                tails.append([lines[f * LEN:(f + 1) * LEN, LEN:] for f in range(4)])
            none = jnp.zeros((LEN, 4 * LEN), jnp.bfloat16)
            above = jnp.concatenate(owns[0] + [none] + tails[0], 1)
            below = jnp.concatenate([none] + owns[1] + tails[1], 1)
            prints = jnp.dot(
                jnp.concatenate(row_weights, 1), jnp.concatenate([above, below], 0),
                preferred_element_type=jnp.float32,
            )
            for region in range(3):
                for f in range(4):
                    at = (region * 4 + f) * LEN
                    foot[region, z, f, 0:tall, :] = prints[:, at:at + LEN]
            return carry

        lax.fori_loop(0, SLICES, slice_body, 0, unroll=8)

    def shade(view):
        rim = RIMS[view]
        tall = LEN + 2 * rim
        backward = orders[view]
        steps = [z + backward * (SLICES - 1 - 2 * z) for z in range(SLICES)]

        def integrate(region, rows):
            through = jnp.ones((8, LEN), jnp.float32)
            depth = jnp.zeros((8, LEN), jnp.float32)
            colors = [jnp.zeros((8, LEN), jnp.float32) for _ in range(3)]
            for z in steps:
                e = foot[region, z, 0, rows, :]
                after = through * jnp.exp(-e)
                weight = through - after
                through = after
                depth += e
                for c in range(3):
                    colors[c] += foot[region, z, 1 + c, rows, :] * weight
            return colors + [depth]

        def row_body(i, carry):
            rows = pl.ds(pl.multiple_of(i * 8, 8), 8)
            rims = integrate(2, rows)
            lefts = jnp.zeros((8, LEN), jnp.float32)
            rights = jnp.zeros((8, LEN), jnp.float32)
            for c in range(4):
                mine = jnp.where((tile_lane >= SLOT) & (tile_lane < 2 * SLOT), rims[c], 0.0)
                lefts += pltpu.roll(mine, (SLOT * c - SLOT) % LEN, 1)
                mine = jnp.where((tile_lane >= 2 * SLOT) & (tile_lane < 3 * SLOT), rims[c], 0.0)
                rights += pltpu.roll(mine, (SLOT * c - 2 * SLOT) % LEN, 1)
            left[view, rows, :] = lefts
            right[view, rows, :] = rights
            first = integrate(0, rows)
            for c in range(4):
                image[view, 0, c, rows, :] = first[c] + jnp.where(tile_lane >= 3 * SLOT, rims[c], 0.0)
            second = integrate(1, rows)
            for c in range(4):
                image[view, 1, c, rows, :] = second[c] + jnp.where(tile_lane < SLOT, rims[c], 0.0)
            return carry

        lax.fori_loop(0, tall // 8, row_body, 0)

    def rim_copies(view):
        rim = RIMS[view]
        top, mid, low = pl.ds(0, rim), pl.ds(rim, LEN), pl.ds(rim + LEN, rim)
        near = pl.ds(0, rim)
        moves = {
            UP_LEFT: (left.at[view, top, :], from_corner.at[view, 0, near, :]),
            UP_RIGHT: (right.at[view, top, :], from_corner.at[view, 1, near, :]),
            DOWN_LEFT: (left.at[view, low, :], from_corner.at[view, 2, near, :]),
            DOWN_RIGHT: (right.at[view, low, :], from_corner.at[view, 3, near, :]),
            ROW_UP: (image.at[view, :, :, top, :], from_row.at[view, 0, :, :, near, :]),
            ROW_DOWN: (image.at[view, :, :, low, :], from_row.at[view, 1, :, :, near, :]),
            COL_LEFT: (left.at[view, mid, :], from_col.at[view, 0]),
            COL_RIGHT: (right.at[view, mid, :], from_col.at[view, 1]),
        }
        return [
            pltpu.make_async_remote_copy(
                src_ref=src, dst_ref=dst,
                send_sem=send_rim.at[view, way], recv_sem=recv_rim.at[view, way],
                device_id=around[way], device_id_type=MESH,
            )
            for way, (src, dst) in moves.items()
        ]

    def fold(view):
        rim = RIMS[view]
        tiles = LEN // 8
        for i in range(tiles):
            rows = slice(rim + i * 8, rim + i * 8 + 8)
            here = slice(i * 8, i * 8 + 8)
            from_right = from_col[view, 0, here, :]
            from_left = from_col[view, 1, here, :]
            above = i * 8 < rim
            below = i * 8 >= LEN - rim
            if above:
                from_right += from_corner[view, 2, here, :]
                from_left += from_corner[view, 3, here, :]
            if below:
                lows = slice(i * 8 - (LEN - rim), i * 8 - (LEN - rim) + 8)
                from_right += from_corner[view, 0, lows, :]
                from_left += from_corner[view, 1, lows, :]
            for c in range(4):
                own = [image[view, b, c, rows, :] for b in range(2)]
                own[0] += jnp.where(
                    tile_lane < SLOT, pltpu.roll(from_left, (-SLOT * c) % LEN, 1), 0.0
                )
                own[1] += jnp.where(
                    tile_lane >= LEN - SLOT,
                    pltpu.roll(from_right, (LEN - SLOT - SLOT * c) % LEN, 1), 0.0,
                )
                for b in range(2):
                    if above:
                        own[b] += from_row[view, 1, b, c, here, :]
                    if below:
                        own[b] += from_row[view, 0, b, c, lows, :]
                    image[view, b, c, rows, :] = own[b]
        for k in range(sections):
            place_of = lax.rem(sign * (k - me) + sections, sections)
            for b in range(2):
                for c in range(4):
                    part = image[
                        view, b, c, pl.ds(rim + k, LEN // sections, stride=sections), :
                    ]
                    sent[view, place_of, b, c] = jnp.exp(-part) if c == 3 else part

    def over(view, near, far):
        mine_first = orders[view] == odd
        weight_near = jnp.where(mine_first, 1.0, far[3])
        weight_far = jnp.where(mine_first, near[3], 1.0)
        return [near[c] * weight_near + far[c] * weight_far for c in range(3)] + [near[3] * far[3]]

    def near_copies(view):
        return [
            pltpu.make_async_remote_copy(
                src_ref=sent.at[view, e], dst_ref=raw.at[view, e - 1],
                send_sem=send_near.at[view, e - 1], recv_sem=recv_near.at[view, e - 1],
                device_id={"depth": partner}, device_id_type=MESH,
            )
            for e in (4, 3, 2, 1)
        ]

    def far_copy(view, e):
        other = lax.rem(me - sign * (sections - e) + 2 * sections, sections)
        slot = lax.rem(me // 2 - other // 2 + sections // 2, sections // 2)
        return pltpu.make_async_remote_copy(
            src_ref=sent.at[view, e], dst_ref=got[view].at[slot],
            send_sem=send_far.at[view, e - 5], recv_sem=recv_far.at[view, slot],
            device_id={"depth": other}, device_id_type=MESH,
        )

    def merge(view):
        for e in (5, 6, 7):
            near_sends[view][e - 5].wait_recv()
            for b in range(2):
                merged = over(
                    view, [sent[view, e, b, c] for c in range(4)], [raw[view, 7 - (e - 1), b, c] for c in range(4)]
                )
                for c in range(4):
                    sent[view, e, b, c] = merged[c]
            far_sends[view].append(far_copy(view, e))
            far_sends[view][-1].start()
        near_sends[view][3].wait_recv()
        for b in range(2):
            merged = over(
                view, [sent[view, 0, b, c] for c in range(4)], [raw[view, 0, b, c] for c in range(4)]
            )
            for c in range(4):
                got[view][0, b, c] = merged[c]

    def composite(view):
        backward = orders[view]
        pairs = sections // 2
        for slot in range(1, pairs):
            pltpu.make_async_remote_copy(
                src_ref=sent.at[view, 5], dst_ref=got[view].at[slot],
                send_sem=send_far.at[view, 0], recv_sem=recv_far.at[view, slot],
                device_id={"depth": partner}, device_id_type=MESH,
            ).wait_recv()
        rows = LEN // sections
        for b in range(2):
            lines = pl.ds(b, rows, stride=2)
            through = jnp.ones((rows, LEN), jnp.float32)
            colors = [jnp.zeros((rows, LEN), jnp.float32) for _ in range(3)]
            for step in range(pairs):
                pair = step + backward * (pairs - 1 - 2 * step)
                slot = lax.rem(pair - me // 2 + pairs, pairs)
                for c in range(3):
                    colors[c] += got[view][slot, b, c] * through
                through = through * got[view][slot, b, 3]
            for c in range(3):
                out[view, c, lines, :] = colors[c]
            out[view, 3, lines, :] = through

    rim_sends, near_sends, far_sends = {}, {}, [[] for _ in range(VIEWS)]

    def settle(view):
        for copy in rim_sends[view]:
            copy.wait()
        fold(view)
        near_sends[view] = near_copies(view)
        for copy in near_sends[view]:
            copy.start()

    for load in loads:
        load.wait()
    def render(view):
        resample(view)
        shade(view)
        if view == 2:
            pl.semaphore_wait(barrier, 8 + sections - 1)
        rim_sends[view] = rim_copies(view)
        for copy in rim_sends[view]:
            copy.start()

    render(2)
    render(1)
    settle(2)
    render(0)
    settle(1)
    merge(2)
    settle(0)
    merge(1)
    composite(2)
    merge(0)
    composite(1)
    composite(0)
    for view in range(VIEWS):
        for copy in near_sends[view] + far_sends[view]:
            copy.wait_send()


def local(density, emission, offsets, view_order, sections, bands, stripes):
    rows, columns = LEN // sections, 2 * LEN
    vmem, smem, hbm = (
        pl.BlockSpec(memory_space=space) for space in (pltpu.VMEM, pltpu.SMEM, pltpu.HBM)
    )
    image = pl.pallas_call(
        functools.partial(kernel, sections, bands, stripes),
        out_shape=jax.ShapeDtypeStruct((VIEWS, 4, 2 * rows, LEN), jnp.float32),
        in_specs=[hbm, hbm, smem, smem],
        out_specs=vmem,
        scratch_shapes=[
            pltpu.VMEM(density.shape, density.dtype),
            pltpu.VMEM(emission.shape, emission.dtype),
            pltpu.VMEM((3, SLICES, 4, TALL, LEN), jnp.float32),
            pltpu.VMEM((VIEWS, 2, 4, TALL, LEN), jnp.float32),
            pltpu.VMEM((VIEWS, TALL, LEN), jnp.float32),
            pltpu.VMEM((VIEWS, TALL, LEN), jnp.float32),
            pltpu.VMEM((VIEWS, 2, 2, 4, RIM, LEN), jnp.float32),
            pltpu.VMEM((VIEWS, 2, LEN, LEN), jnp.float32),
            pltpu.VMEM((VIEWS, 4, RIM, LEN), jnp.float32),
            pltpu.VMEM((VIEWS, sections, 2, 4, rows, LEN), jnp.float32),
            pltpu.VMEM((VIEWS, 4, 2, 4, rows, LEN), jnp.float32),
            pltpu.VMEM((sections // 2, 2, 4, rows, LEN), jnp.float32),
            pltpu.VMEM((sections // 2, 2, 4, rows, LEN), jnp.float32),
            pltpu.VMEM((sections // 2, 2, 4, rows, LEN), jnp.float32),
            pltpu.SemaphoreType.DMA((2,)),
            pltpu.SemaphoreType.DMA((VIEWS, 8)),
            pltpu.SemaphoreType.DMA((VIEWS, 8)),
            pltpu.SemaphoreType.DMA((VIEWS, 4)),
            pltpu.SemaphoreType.DMA((VIEWS, 4)),
            pltpu.SemaphoreType.DMA((VIEWS, 4)),
            pltpu.SemaphoreType.DMA((VIEWS, 4)),
        ],
        compiler_params=pltpu.CompilerParams(
            collective_id=0, has_side_effects=True, vmem_limit_bytes=50 * 1024 * 1024
        ),
    )(
        *(
            pltpu.with_memory_space_constraint(x, pltpu.HBM)
            for x in (
                density, emission,
                offsets.transpose(1, 2, 3, 4, 0).reshape(2, 2, VIEWS), view_order.reshape(-1),
            )
        )
    )
    return image.reshape(VIEWS, 4, rows, 1, columns)


def solution(mesh):
    return jax.shard_map(
        functools.partial(
            local, sections=mesh.shape["depth"], bands=mesh.shape["row"], stripes=mesh.shape["col"]
        ),
        mesh=mesh,
        in_specs=(
            P("depth", "row", "col"),
            P(None, "depth", "row", "col"),
            P(None, None, "depth", "row", "col"),
            P(None, "row"),
        ),
        out_specs=P(None, None, "row", "depth", "col"),
        check_vma=False,
    )
```

```python
import functools

import jax
import jax.numpy as jnp
from jax import lax
from jax.experimental import pallas as pl
from jax.experimental.pallas import tpu as pltpu
from jax.sharding import PartitionSpec as P

MESH = pl.DeviceIdType.MESH
VIEWS = 3
MARGIN = 16
JIT = 8
SLICES = 8
LEN = 128
SHEAR_ROWS = (0.75, -0.5, 0.25)
SHEAR_COLS = (-0.25, 0.625, -0.875)
RIMS = tuple(
    -(-int(abs(a) * (MARGIN - 2) * (SLICES - 1) / SLICES + 1 + JIT) // 8) * 8 for a in SHEAR_ROWS
)
RIM = max(RIMS)
TALL = LEN + 2 * RIM
SLOT = 32

ROW_UP, ROW_DOWN, COL_LEFT, COL_RIGHT, UP_LEFT, UP_RIGHT, DOWN_LEFT, DOWN_RIGHT = range(8)


def shift_of(rate, z):
    return rate * (MARGIN - 2) / SLICES * (2.0 * z - (SLICES - 1))


def tent(distance):
    return jnp.maximum(0.0, 1.0 - jnp.abs(distance)).astype(jnp.bfloat16)


def kernel(
    sections, bands, stripes,
    density_hbm, emission_hbm, offsets, orders, out,
    density, emission, foot, image, left, right,
    from_row, from_col, from_corner, sent, raw, got_0, got_1, got_2,
    load_sem, send_rim, recv_rim, send_near, recv_near, send_far, recv_far,
):
    loads = []
    for part in range(SLICES // 2):
        zs = slice(2 * part, 2 * part + 2)
        loads.append((
            pltpu.make_async_copy(density_hbm.at[zs], density.at[zs], load_sem.at[0, part]),
            pltpu.make_async_copy(emission_hbm.at[:, zs], emission.at[:, zs], load_sem.at[1, part]),
        ))
        for load in loads[part]:
            load.start()
    got = (got_0, got_1, got_2)
    me = lax.axis_index("depth")
    odd = lax.rem(me, 2)
    sign = 1 - 2 * odd
    partner = me + sign
    band = lax.axis_index("row")
    stripe = lax.axis_index("col")

    def place(drow, dcol):
        return {
            "row": lax.rem(band + drow + bands, bands),
            "col": lax.rem(stripe + dcol + stripes, stripes),
        }

    around = {
        ROW_UP: place(-1, 0), ROW_DOWN: place(1, 0), COL_LEFT: place(0, -1), COL_RIGHT: place(0, 1),
        UP_LEFT: place(-1, -1), UP_RIGHT: place(-1, 1), DOWN_LEFT: place(1, -1), DOWN_RIGHT: place(1, 1),
    }
    barrier = pltpu.get_barrier_semaphore()
    for device in around.values():
        pl.semaphore_signal(barrier, inc=1, device_id=device, device_id_type=MESH)
    for hop in range(1, sections):
        pl.semaphore_signal(
            barrier, inc=1, device_id={"depth": lax.rem(me + hop, sections)}, device_id_type=MESH
        )

    lane = lax.broadcasted_iota(jnp.int32, (LEN, 2 * LEN), 1)
    cell = lax.broadcasted_iota(jnp.int32, (LEN, 2 * LEN), 0)
    tail = lane - LEN
    nowhere = -4096
    column = (
        jnp.where(lane < LEN, lane, jnp.where(tail < SLOT, tail + LEN,
                  jnp.where(tail < 2 * SLOT, tail - 2 * SLOT, nowhere))),
        jnp.where(lane < LEN, lane, jnp.where(tail < 2 * SLOT, nowhere,
                  jnp.where(tail < 3 * SLOT, tail + LEN - 2 * SLOT, tail - LEN))),
    )
    col_base = [(c - cell).astype(jnp.float32) for c in column]
    tile_lane = lax.broadcasted_iota(jnp.int32, (8, LEN), 1)

    def resample(view, first):
        rim = RIMS[view]
        tall = LEN + 2 * rim
        row_base = (
            lax.broadcasted_iota(jnp.int32, (tall, LEN), 0) - rim
            - lax.broadcasted_iota(jnp.int32, (tall, LEN), 1)
        ).astype(jnp.float32)

        def slice_body(z):
            zf = jnp.float32(z)
            owns, tails, row_weights = [], [], []
            for b in range(2):
                oy = offsets[0, b, view].astype(jnp.float32)
                ox = offsets[1, b, view].astype(jnp.float32)
                cols = slice(b * LEN, (b + 1) * LEN)
                cells = jnp.concatenate(
                    [density[z, :, cols]] + [emission[c, z, :, cols] for c in range(3)], 0
                )
                col_weights = tent(col_base[b] - (ox + shift_of(SHEAR_COLS[view], zf)))
                lines = jnp.dot(
                    cells, col_weights, preferred_element_type=jnp.float32
                ).astype(jnp.bfloat16)
                row_weights.append(tent(row_base - (oy + shift_of(SHEAR_ROWS[view], zf))))
                owns.append([lines[f * LEN:(f + 1) * LEN, :LEN] for f in range(4)])
                tails.append([lines[f * LEN:(f + 1) * LEN, LEN:] for f in range(4)])
            none = jnp.zeros((LEN, 4 * LEN), jnp.bfloat16)
            above = jnp.concatenate(owns[0] + [none] + tails[0], 1)
            below = jnp.concatenate([none] + owns[1] + tails[1], 1)
            prints = jnp.dot(
                jnp.concatenate(row_weights, 1), jnp.concatenate([above, below], 0),
                preferred_element_type=jnp.float32,
            )
            for region in range(3):
                for f in range(4):
                    at = (region * 4 + f) * LEN
                    foot[region, z, f, 0:tall, :] = prints[:, at:at + LEN]

        for z in range(SLICES):
            if first and z % 2 == 0:
                for load in loads[z // 2]:
                    load.wait()
            slice_body(z)

    def shade(view):
        rim = RIMS[view]
        tall = LEN + 2 * rim
        backward = orders[view]
        steps = [z + backward * (SLICES - 1 - 2 * z) for z in range(SLICES)]

        def integrate(region, rows):
            through = jnp.ones((8, LEN), jnp.float32)
            depth = jnp.zeros((8, LEN), jnp.float32)
            colors = [jnp.zeros((8, LEN), jnp.float32) for _ in range(3)]
            for z in steps:
                e = foot[region, z, 0, rows, :]
                after = through * jnp.exp(-e)
                weight = through - after
                through = after
                depth += e
                for c in range(3):
                    colors[c] += foot[region, z, 1 + c, rows, :] * weight
            return colors + [depth]

        def row_body(i, carry):
            rows = pl.ds(pl.multiple_of(i * 8, 8), 8)
            rims = integrate(2, rows)
            lefts = jnp.zeros((8, LEN), jnp.float32)
            rights = jnp.zeros((8, LEN), jnp.float32)
            for c in range(4):
                mine = jnp.where((tile_lane >= SLOT) & (tile_lane < 2 * SLOT), rims[c], 0.0)
                lefts += pltpu.roll(mine, (SLOT * c - SLOT) % LEN, 1)
                mine = jnp.where((tile_lane >= 2 * SLOT) & (tile_lane < 3 * SLOT), rims[c], 0.0)
                rights += pltpu.roll(mine, (SLOT * c - 2 * SLOT) % LEN, 1)
            left[view, rows, :] = lefts
            right[view, rows, :] = rights
            first = integrate(0, rows)
            for c in range(4):
                image[view, 0, c, rows, :] = first[c] + jnp.where(tile_lane >= 3 * SLOT, rims[c], 0.0)
            second = integrate(1, rows)
            for c in range(4):
                image[view, 1, c, rows, :] = second[c] + jnp.where(tile_lane < SLOT, rims[c], 0.0)
            return carry

        lax.fori_loop(0, tall // 8, row_body, 0)

    def rim_copies(view):
        rim = RIMS[view]
        top, mid, low = pl.ds(0, rim), pl.ds(rim, LEN), pl.ds(rim + LEN, rim)
        near = pl.ds(0, rim)
        moves = {
            UP_LEFT: (left.at[view, top, :], from_corner.at[view, 0, near, :]),
            UP_RIGHT: (right.at[view, top, :], from_corner.at[view, 1, near, :]),
            DOWN_LEFT: (left.at[view, low, :], from_corner.at[view, 2, near, :]),
            DOWN_RIGHT: (right.at[view, low, :], from_corner.at[view, 3, near, :]),
            ROW_UP: (image.at[view, :, :, top, :], from_row.at[view, 0, :, :, near, :]),
            ROW_DOWN: (image.at[view, :, :, low, :], from_row.at[view, 1, :, :, near, :]),
            COL_LEFT: (left.at[view, mid, :], from_col.at[view, 0]),
            COL_RIGHT: (right.at[view, mid, :], from_col.at[view, 1]),
        }
        return [
            pltpu.make_async_remote_copy(
                src_ref=src, dst_ref=dst,
                send_sem=send_rim.at[view, way], recv_sem=recv_rim.at[view, way],
                device_id=around[way], device_id_type=MESH,
            )
            for way, (src, dst) in moves.items()
        ]

    def fold(view):
        rim = RIMS[view]
        tiles = LEN // 8
        for i in range(tiles):
            rows = slice(rim + i * 8, rim + i * 8 + 8)
            here = slice(i * 8, i * 8 + 8)
            from_right = from_col[view, 0, here, :]
            from_left = from_col[view, 1, here, :]
            above = i * 8 < rim
            below = i * 8 >= LEN - rim
            if above:
                from_right += from_corner[view, 2, here, :]
                from_left += from_corner[view, 3, here, :]
            if below:
                lows = slice(i * 8 - (LEN - rim), i * 8 - (LEN - rim) + 8)
                from_right += from_corner[view, 0, lows, :]
                from_left += from_corner[view, 1, lows, :]
            for c in range(4):
                own = [image[view, b, c, rows, :] for b in range(2)]
                own[0] += jnp.where(
                    tile_lane < SLOT, pltpu.roll(from_left, (-SLOT * c) % LEN, 1), 0.0
                )
                own[1] += jnp.where(
                    tile_lane >= LEN - SLOT,
                    pltpu.roll(from_right, (LEN - SLOT - SLOT * c) % LEN, 1), 0.0,
                )
                for b in range(2):
                    if above:
                        own[b] += from_row[view, 1, b, c, here, :]
                    if below:
                        own[b] += from_row[view, 0, b, c, lows, :]
                    image[view, b, c, rows, :] = own[b]
        for k in range(sections):
            place_of = lax.rem(sign * (k - me) + sections, sections)
            for b in range(2):
                for c in range(4):
                    part = image[
                        view, b, c, pl.ds(rim + k, LEN // sections, stride=sections), :
                    ]
                    sent[view, place_of, b, c] = jnp.exp(-part) if c == 3 else part

    def over(view, near, far):
        mine_first = orders[view] == odd
        weight_near = jnp.where(mine_first, 1.0, far[3])
        weight_far = jnp.where(mine_first, near[3], 1.0)
        return [near[c] * weight_near + far[c] * weight_far for c in range(3)] + [near[3] * far[3]]

    def near_copies(view):
        return [
            pltpu.make_async_remote_copy(
                src_ref=sent.at[view, e], dst_ref=raw.at[view, e - 1],
                send_sem=send_near.at[view, e - 1], recv_sem=recv_near.at[view, e - 1],
                device_id={"depth": partner}, device_id_type=MESH,
            )
            for e in (4, 3, 2, 1)
        ]

    def far_copy(view, e):
        other = lax.rem(me - sign * (sections - e) + 2 * sections, sections)
        slot = lax.rem(me // 2 - other // 2 + sections // 2, sections // 2)
        return pltpu.make_async_remote_copy(
            src_ref=sent.at[view, e], dst_ref=got[view].at[slot],
            send_sem=send_far.at[view, e - 5], recv_sem=recv_far.at[view, slot],
            device_id={"depth": other}, device_id_type=MESH,
        )

    def merge(view):
        for e in (5, 6, 7):
            near_sends[view][e - 5].wait_recv()
            for b in range(2):
                merged = over(
                    view, [sent[view, e, b, c] for c in range(4)], [raw[view, 7 - (e - 1), b, c] for c in range(4)]
                )
                for c in range(4):
                    sent[view, e, b, c] = merged[c]
            far_sends[view].append(far_copy(view, e))
            far_sends[view][-1].start()
        near_sends[view][3].wait_recv()
        for b in range(2):
            merged = over(
                view, [sent[view, 0, b, c] for c in range(4)], [raw[view, 0, b, c] for c in range(4)]
            )
            for c in range(4):
                got[view][0, b, c] = merged[c]

    def composite(view):
        backward = orders[view]
        pairs = sections // 2
        for slot in range(1, pairs):
            pltpu.make_async_remote_copy(
                src_ref=sent.at[view, 5], dst_ref=got[view].at[slot],
                send_sem=send_far.at[view, 0], recv_sem=recv_far.at[view, slot],
                device_id={"depth": partner}, device_id_type=MESH,
            ).wait_recv()
        rows = LEN // sections
        for b in range(2):
            lines = pl.ds(b, rows, stride=2)
            through = jnp.ones((rows, LEN), jnp.float32)
            colors = [jnp.zeros((rows, LEN), jnp.float32) for _ in range(3)]
            for step in range(pairs):
                pair = step + backward * (pairs - 1 - 2 * step)
                slot = lax.rem(pair - me // 2 + pairs, pairs)
                for c in range(3):
                    colors[c] += got[view][slot, b, c] * through
                through = through * got[view][slot, b, 3]
            for c in range(3):
                out[view, c, lines, :] = colors[c]
            out[view, 3, lines, :] = through

    rim_sends, near_sends, far_sends = {}, {}, [[] for _ in range(VIEWS)]

    def settle(view):
        for copy in rim_sends[view]:
            copy.wait()
        fold(view)
        near_sends[view] = near_copies(view)
        for copy in near_sends[view]:
            copy.start()

    def render(view):
        resample(view, view == 2)
        shade(view)
        if view == 2:
            pl.semaphore_wait(barrier, 8 + sections - 1)
        rim_sends[view] = rim_copies(view)
        for copy in rim_sends[view]:
            copy.start()

    render(2)
    render(1)
    settle(2)
    render(0)
    settle(1)
    merge(2)
    settle(0)
    merge(1)
    merge(0)
    composite(2)
    composite(1)
    composite(0)
    for view in range(VIEWS):
        for copy in near_sends[view] + far_sends[view]:
            copy.wait_send()


def local(density, emission, offsets, view_order, sections, bands, stripes):
    rows, columns = LEN // sections, 2 * LEN
    vmem, smem, hbm = (
        pl.BlockSpec(memory_space=space) for space in (pltpu.VMEM, pltpu.SMEM, pltpu.HBM)
    )
    image = pl.pallas_call(
        functools.partial(kernel, sections, bands, stripes),
        out_shape=jax.ShapeDtypeStruct((VIEWS, 4, 2 * rows, LEN), jnp.float32),
        in_specs=[hbm, hbm, smem, smem],
        out_specs=vmem,
        scratch_shapes=[
            pltpu.VMEM(density.shape, density.dtype),
            pltpu.VMEM(emission.shape, emission.dtype),
            pltpu.VMEM((3, SLICES, 4, TALL, LEN), jnp.float32),
            pltpu.VMEM((VIEWS, 2, 4, TALL, LEN), jnp.float32),
            pltpu.VMEM((VIEWS, TALL, LEN), jnp.float32),
            pltpu.VMEM((VIEWS, TALL, LEN), jnp.float32),
            pltpu.VMEM((VIEWS, 2, 2, 4, RIM, LEN), jnp.float32),
            pltpu.VMEM((VIEWS, 2, LEN, LEN), jnp.float32),
            pltpu.VMEM((VIEWS, 4, RIM, LEN), jnp.float32),
            pltpu.VMEM((VIEWS, sections, 2, 4, rows, LEN), jnp.float32),
            pltpu.VMEM((VIEWS, 4, 2, 4, rows, LEN), jnp.float32),
            pltpu.VMEM((sections // 2, 2, 4, rows, LEN), jnp.float32),
            pltpu.VMEM((sections // 2, 2, 4, rows, LEN), jnp.float32),
            pltpu.VMEM((sections // 2, 2, 4, rows, LEN), jnp.float32),
            pltpu.SemaphoreType.DMA((2, SLICES // 2)),
            pltpu.SemaphoreType.DMA((VIEWS, 8)),
            pltpu.SemaphoreType.DMA((VIEWS, 8)),
            pltpu.SemaphoreType.DMA((VIEWS, 4)),
            pltpu.SemaphoreType.DMA((VIEWS, 4)),
            pltpu.SemaphoreType.DMA((VIEWS, 4)),
            pltpu.SemaphoreType.DMA((VIEWS, 4)),
        ],
        compiler_params=pltpu.CompilerParams(
            collective_id=0, has_side_effects=True, vmem_limit_bytes=50 * 1024 * 1024
        ),
    )(
        *(
            pltpu.with_memory_space_constraint(x, pltpu.HBM)
            for x in (
                density, emission,
                offsets.transpose(1, 2, 3, 4, 0).reshape(2, 2, VIEWS), view_order.reshape(-1),
            )
        )
    )
    return image.reshape(VIEWS, 4, rows, 1, columns)


def solution(mesh):
    return jax.shard_map(
        functools.partial(
            local, sections=mesh.shape["depth"], bands=mesh.shape["row"], stripes=mesh.shape["col"]
        ),
        mesh=mesh,
        in_specs=(
            P("depth", "row", "col"),
            P(None, "depth", "row", "col"),
            P(None, None, "depth", "row", "col"),
            P(None, "row"),
        ),
        out_specs=P(None, None, "row", "depth", "col"),
        check_vma=False,
    )
```

```python
import functools

import jax
import jax.numpy as jnp
from jax import lax
from jax.experimental import pallas as pl
from jax.experimental.pallas import tpu as pltpu
from jax.sharding import PartitionSpec as P

MESH = pl.DeviceIdType.MESH
VIEWS = 3
MARGIN = 16
JIT = 8
SLICES = 8
LEN = 128
SHEAR_ROWS = (0.75, -0.5, 0.25)
SHEAR_COLS = (-0.25, 0.625, -0.875)
RIMS = tuple(
    -(-int(abs(a) * (MARGIN - 2) * (SLICES - 1) / SLICES + 1 + JIT) // 8) * 8 for a in SHEAR_ROWS
)
RIM = max(RIMS)
TALL = LEN + 2 * RIM
LOG2_E = 1.4426950408889634
SLOT = 32

ROW_UP, ROW_DOWN, COL_LEFT, COL_RIGHT, UP_LEFT, UP_RIGHT, DOWN_LEFT, DOWN_RIGHT = range(8)


def shift_of(rate, z):
    return rate * (MARGIN - 2) / SLICES * (2.0 * z - (SLICES - 1))


def tent(distance):
    return jnp.maximum(0.0, 1.0 - jnp.abs(distance)).astype(jnp.bfloat16)


def kernel(
    sections, bands, stripes,
    density_hbm, emission_hbm, offsets, orders, out,
    density, emission, foot, image, left, right,
    from_row, from_col, from_corner, sent, raw, got_0, got_1, got_2,
    load_sem, send_rim, recv_rim, send_near, recv_near, send_far, recv_far,
):
    loads = (
        pltpu.make_async_copy(density_hbm, density, load_sem.at[0]),
        pltpu.make_async_copy(emission_hbm, emission, load_sem.at[1]),
    )
    for load in loads:
        load.start()
    got = (got_0, got_1, got_2)
    me = lax.axis_index("depth")
    odd = lax.rem(me, 2)
    sign = 1 - 2 * odd
    partner = me + sign
    band = lax.axis_index("row")
    stripe = lax.axis_index("col")

    def place(drow, dcol):
        return {
            "row": lax.rem(band + drow + bands, bands),
            "col": lax.rem(stripe + dcol + stripes, stripes),
        }

    around = {
        ROW_UP: place(-1, 0), ROW_DOWN: place(1, 0), COL_LEFT: place(0, -1), COL_RIGHT: place(0, 1),
        UP_LEFT: place(-1, -1), UP_RIGHT: place(-1, 1), DOWN_LEFT: place(1, -1), DOWN_RIGHT: place(1, 1),
    }
    barrier = pltpu.get_barrier_semaphore()
    for device in around.values():
        pl.semaphore_signal(barrier, inc=1, device_id=device, device_id_type=MESH)
    for hop in range(1, sections):
        pl.semaphore_signal(
            barrier, inc=1, device_id={"depth": lax.rem(me + hop, sections)}, device_id_type=MESH
        )

    lane = lax.broadcasted_iota(jnp.int32, (LEN, 2 * LEN), 1)
    cell = lax.broadcasted_iota(jnp.int32, (LEN, 2 * LEN), 0)
    tail = lane - LEN
    nowhere = -4096
    column = (
        jnp.where(lane < LEN, lane, jnp.where(tail < SLOT, tail + LEN,
                  jnp.where(tail < 2 * SLOT, tail - 2 * SLOT, nowhere))),
        jnp.where(lane < LEN, lane, jnp.where(tail < 2 * SLOT, nowhere,
                  jnp.where(tail < 3 * SLOT, tail + LEN - 2 * SLOT, tail - LEN))),
    )
    col_base = [(c - cell).astype(jnp.float32) for c in column]
    tile_lane = lax.broadcasted_iota(jnp.int32, (8, LEN), 1)

    def resample(view):
        rim = RIMS[view]
        tall = LEN + 2 * rim
        row_base = (
            lax.broadcasted_iota(jnp.int32, (tall, LEN), 0) - rim
            - lax.broadcasted_iota(jnp.int32, (tall, LEN), 1)
        ).astype(jnp.float32)

        def slice_body(z, carry):
            zf = z.astype(jnp.float32)
            owns, tails, row_weights = [], [], []
            for b in range(2):
                oy = offsets[0, b, view].astype(jnp.float32)
                ox = offsets[1, b, view].astype(jnp.float32)
                cols = slice(b * LEN, (b + 1) * LEN)
                cells = jnp.concatenate(
                    [density[z, :, cols]] + [emission[c, z, :, cols] for c in range(3)], 0
                )
                col_weights = tent(col_base[b] - (ox + shift_of(SHEAR_COLS[view], zf)))
                lines = jnp.dot(
                    cells, col_weights, preferred_element_type=jnp.float32
                ).astype(jnp.bfloat16)
                row_weights.append(tent(row_base - (oy + shift_of(SHEAR_ROWS[view], zf))))
                owns.append([lines[f * LEN:(f + 1) * LEN, :LEN] for f in range(4)])
                tails.append([lines[f * LEN:(f + 1) * LEN, LEN:] for f in range(4)])
            none = jnp.zeros((LEN, 4 * LEN), jnp.bfloat16)
            above = jnp.concatenate(owns[0] + [none] + tails[0], 1)
            below = jnp.concatenate([none] + owns[1] + tails[1], 1)
            prints = jnp.dot(
                jnp.concatenate(row_weights, 1), jnp.concatenate([above, below], 0),
                preferred_element_type=jnp.float32,
            )
            for region in range(3):
                for f in range(4):
                    at = (region * 4 + f) * LEN
                    foot[region, z, f, 0:tall, :] = prints[:, at:at + LEN]
            return carry

        lax.fori_loop(0, SLICES, slice_body, 0, unroll=8)

    def shade(view):
        rim = RIMS[view]
        tall = LEN + 2 * rim
        backward = orders[view]
        steps = [z + backward * (SLICES - 1 - 2 * z) for z in range(SLICES)]

        def integrate(region, rows):
            through = jnp.ones((8, LEN), jnp.float32)
            depth = jnp.zeros((8, LEN), jnp.float32)
            colors = [jnp.zeros((8, LEN), jnp.float32) for _ in range(3)]
            for z in steps:
                e = foot[region, z, 0, rows, :]
                after = through * jnp.exp2(e * -LOG2_E)
                weight = through - after
                through = after
                depth += e
                for c in range(3):
                    colors[c] += foot[region, z, 1 + c, rows, :] * weight
            return colors + [depth]

        def row_body(i, carry):
            rows = pl.ds(pl.multiple_of(i * 8, 8), 8)
            rims = integrate(2, rows)
            lefts = jnp.zeros((8, LEN), jnp.float32)
            rights = jnp.zeros((8, LEN), jnp.float32)
            for c in range(4):
                mine = jnp.where((tile_lane >= SLOT) & (tile_lane < 2 * SLOT), rims[c], 0.0)
                lefts += pltpu.roll(mine, (SLOT * c - SLOT) % LEN, 1)
                mine = jnp.where((tile_lane >= 2 * SLOT) & (tile_lane < 3 * SLOT), rims[c], 0.0)
                rights += pltpu.roll(mine, (SLOT * c - 2 * SLOT) % LEN, 1)
            left[view, rows, :] = lefts
            right[view, rows, :] = rights
            first = integrate(0, rows)
            for c in range(4):
                image[view, 0, c, rows, :] = first[c] + jnp.where(tile_lane >= 3 * SLOT, rims[c], 0.0)
            second = integrate(1, rows)
            for c in range(4):
                image[view, 1, c, rows, :] = second[c] + jnp.where(tile_lane < SLOT, rims[c], 0.0)
            return carry

        lax.fori_loop(0, tall // 8, row_body, 0)

    def rim_copies(view):
        rim = RIMS[view]
        top, mid, low = pl.ds(0, rim), pl.ds(rim, LEN), pl.ds(rim + LEN, rim)
        near = pl.ds(0, rim)
        moves = {
            UP_LEFT: (left.at[view, top, :], from_corner.at[view, 0, near, :]),
            UP_RIGHT: (right.at[view, top, :], from_corner.at[view, 1, near, :]),
            DOWN_LEFT: (left.at[view, low, :], from_corner.at[view, 2, near, :]),
            DOWN_RIGHT: (right.at[view, low, :], from_corner.at[view, 3, near, :]),
            ROW_UP: (image.at[view, :, :, top, :], from_row.at[view, 0, :, :, near, :]),
            ROW_DOWN: (image.at[view, :, :, low, :], from_row.at[view, 1, :, :, near, :]),
            COL_LEFT: (left.at[view, mid, :], from_col.at[view, 0]),
            COL_RIGHT: (right.at[view, mid, :], from_col.at[view, 1]),
        }
        return [
            pltpu.make_async_remote_copy(
                src_ref=src, dst_ref=dst,
                send_sem=send_rim.at[view, way], recv_sem=recv_rim.at[view, way],
                device_id=around[way], device_id_type=MESH,
            )
            for way, (src, dst) in moves.items()
        ]

    def fold(view):
        rim = RIMS[view]
        tiles = LEN // 8
        for i in range(tiles):
            rows = slice(rim + i * 8, rim + i * 8 + 8)
            here = slice(i * 8, i * 8 + 8)
            from_right = from_col[view, 0, here, :]
            from_left = from_col[view, 1, here, :]
            above = i * 8 < rim
            below = i * 8 >= LEN - rim
            if above:
                from_right += from_corner[view, 2, here, :]
                from_left += from_corner[view, 3, here, :]
            if below:
                lows = slice(i * 8 - (LEN - rim), i * 8 - (LEN - rim) + 8)
                from_right += from_corner[view, 0, lows, :]
                from_left += from_corner[view, 1, lows, :]
            for c in range(4):
                own = [image[view, b, c, rows, :] for b in range(2)]
                own[0] += jnp.where(
                    tile_lane < SLOT, pltpu.roll(from_left, (-SLOT * c) % LEN, 1), 0.0
                )
                own[1] += jnp.where(
                    tile_lane >= LEN - SLOT,
                    pltpu.roll(from_right, (LEN - SLOT - SLOT * c) % LEN, 1), 0.0,
                )
                for b in range(2):
                    if above:
                        own[b] += from_row[view, 1, b, c, here, :]
                    if below:
                        own[b] += from_row[view, 0, b, c, lows, :]
                    image[view, b, c, rows, :] = own[b]
        for k in range(sections):
            place_of = lax.rem(sign * (k - me) + sections, sections)
            for b in range(2):
                for c in range(4):
                    part = image[
                        view, b, c, pl.ds(rim + k, LEN // sections, stride=sections), :
                    ]
                    sent[view, place_of, b, c] = jnp.exp(-part) if c == 3 else part

    def over(view, near, far):
        mine_first = orders[view] == odd
        weight_near = jnp.where(mine_first, 1.0, far[3])
        weight_far = jnp.where(mine_first, near[3], 1.0)
        return [near[c] * weight_near + far[c] * weight_far for c in range(3)] + [near[3] * far[3]]

    def near_copies(view):
        return [
            pltpu.make_async_remote_copy(
                src_ref=sent.at[view, e], dst_ref=raw.at[view, e - 1],
                send_sem=send_near.at[view, e - 1], recv_sem=recv_near.at[view, e - 1],
                device_id={"depth": partner}, device_id_type=MESH,
            )
            for e in (4, 3, 2, 1)
        ]

    def far_copy(view, e):
        other = lax.rem(me - sign * (sections - e) + 2 * sections, sections)
        slot = lax.rem(me // 2 - other // 2 + sections // 2, sections // 2)
        return pltpu.make_async_remote_copy(
            src_ref=sent.at[view, e], dst_ref=got[view].at[slot],
            send_sem=send_far.at[view, e - 5], recv_sem=recv_far.at[view, slot],
            device_id={"depth": other}, device_id_type=MESH,
        )

    def merge(view):
        for e in (5, 6, 7):
            near_sends[view][e - 5].wait_recv()
            for b in range(2):
                merged = over(
                    view, [sent[view, e, b, c] for c in range(4)], [raw[view, 7 - (e - 1), b, c] for c in range(4)]
                )
                for c in range(4):
                    sent[view, e, b, c] = merged[c]
            far_sends[view].append(far_copy(view, e))
            far_sends[view][-1].start()
        near_sends[view][3].wait_recv()
        for b in range(2):
            merged = over(
                view, [sent[view, 0, b, c] for c in range(4)], [raw[view, 0, b, c] for c in range(4)]
            )
            for c in range(4):
                got[view][0, b, c] = merged[c]

    def composite(view):
        backward = orders[view]
        pairs = sections // 2
        for slot in range(1, pairs):
            pltpu.make_async_remote_copy(
                src_ref=sent.at[view, 5], dst_ref=got[view].at[slot],
                send_sem=send_far.at[view, 0], recv_sem=recv_far.at[view, slot],
                device_id={"depth": partner}, device_id_type=MESH,
            ).wait_recv()
        rows = LEN // sections
        for b in range(2):
            lines = pl.ds(b, rows, stride=2)
            through = jnp.ones((rows, LEN), jnp.float32)
            colors = [jnp.zeros((rows, LEN), jnp.float32) for _ in range(3)]
            for step in range(pairs):
                pair = step + backward * (pairs - 1 - 2 * step)
                slot = lax.rem(pair - me // 2 + pairs, pairs)
                for c in range(3):
                    colors[c] += got[view][slot, b, c] * through
                through = through * got[view][slot, b, 3]
            for c in range(3):
                out[view, c, lines, :] = colors[c]
            out[view, 3, lines, :] = through

    rim_sends, near_sends, far_sends = {}, {}, [[] for _ in range(VIEWS)]

    def settle(view):
        for copy in rim_sends[view]:
            copy.wait()
        fold(view)
        near_sends[view] = near_copies(view)
        for copy in near_sends[view]:
            copy.start()

    for load in loads:
        load.wait()
    def render(view):
        resample(view)
        shade(view)
        if view == 2:
            pl.semaphore_wait(barrier, 8 + sections - 1)
        rim_sends[view] = rim_copies(view)
        for copy in rim_sends[view]:
            copy.start()

    render(2)
    render(1)
    settle(2)
    render(0)
    settle(1)
    merge(2)
    settle(0)
    merge(1)
    composite(2)
    merge(0)
    composite(1)
    composite(0)
    for view in range(VIEWS):
        for copy in near_sends[view] + far_sends[view]:
            copy.wait_send()


def local(density, emission, offsets, view_order, sections, bands, stripes):
    rows, columns = LEN // sections, 2 * LEN
    vmem, smem, hbm = (
        pl.BlockSpec(memory_space=space) for space in (pltpu.VMEM, pltpu.SMEM, pltpu.HBM)
    )
    image = pl.pallas_call(
        functools.partial(kernel, sections, bands, stripes),
        out_shape=jax.ShapeDtypeStruct((VIEWS, 4, 2 * rows, LEN), jnp.float32),
        in_specs=[hbm, hbm, smem, smem],
        out_specs=vmem,
        scratch_shapes=[
            pltpu.VMEM(density.shape, density.dtype),
            pltpu.VMEM(emission.shape, emission.dtype),
            pltpu.VMEM((3, SLICES, 4, TALL, LEN), jnp.float32),
            pltpu.VMEM((VIEWS, 2, 4, TALL, LEN), jnp.float32),
            pltpu.VMEM((VIEWS, TALL, LEN), jnp.float32),
            pltpu.VMEM((VIEWS, TALL, LEN), jnp.float32),
            pltpu.VMEM((VIEWS, 2, 2, 4, RIM, LEN), jnp.float32),
            pltpu.VMEM((VIEWS, 2, LEN, LEN), jnp.float32),
            pltpu.VMEM((VIEWS, 4, RIM, LEN), jnp.float32),
            pltpu.VMEM((VIEWS, sections, 2, 4, rows, LEN), jnp.float32),
            pltpu.VMEM((VIEWS, 4, 2, 4, rows, LEN), jnp.float32),
            pltpu.VMEM((sections // 2, 2, 4, rows, LEN), jnp.float32),
            pltpu.VMEM((sections // 2, 2, 4, rows, LEN), jnp.float32),
            pltpu.VMEM((sections // 2, 2, 4, rows, LEN), jnp.float32),
            pltpu.SemaphoreType.DMA((2,)),
            pltpu.SemaphoreType.DMA((VIEWS, 8)),
            pltpu.SemaphoreType.DMA((VIEWS, 8)),
            pltpu.SemaphoreType.DMA((VIEWS, 4)),
            pltpu.SemaphoreType.DMA((VIEWS, 4)),
            pltpu.SemaphoreType.DMA((VIEWS, 4)),
            pltpu.SemaphoreType.DMA((VIEWS, 4)),
        ],
        compiler_params=pltpu.CompilerParams(
            collective_id=0, has_side_effects=True, vmem_limit_bytes=50 * 1024 * 1024
        ),
    )(
        *(
            pltpu.with_memory_space_constraint(x, pltpu.HBM)
            for x in (
                density, emission,
                offsets.transpose(1, 2, 3, 4, 0).reshape(2, 2, VIEWS), view_order.reshape(-1),
            )
        )
    )
    return image.reshape(VIEWS, 4, rows, 1, columns)


def solution(mesh):
    return jax.shard_map(
        functools.partial(
            local, sections=mesh.shape["depth"], bands=mesh.shape["row"], stripes=mesh.shape["col"]
        ),
        mesh=mesh,
        in_specs=(
            P("depth", "row", "col"),
            P(None, "depth", "row", "col"),
            P(None, None, "depth", "row", "col"),
            P(None, "row"),
        ),
        out_specs=P(None, None, "row", "depth", "col"),
        check_vma=False,
    )
```
